32 devices in a mesh: gx: 4 (over x, core), gy: 8 (over z, y).
Axes of the slice: x: 2, y: 2, z: 4, core: 2. Of those that a mesh axis runs over, the one named last changes fastest.
Arguments:
- source: bfloat16 [16, 512, 256], P(None, ('gx', 'gy')), may hold values from -6 to 6
- leaf_flux: bfloat16 [32768, 256], P(('gx', 'gy')), may hold values from -0.375 to 0.375
- leaf_particular: bfloat16 [131072, 256], P(('gx', 'gy')), may hold values from -0.375 to 0.375
- leaf_lift: bfloat16 [32768, 256], P(('gx', 'gy')), may hold values from -0.75 to 0.75
- box_up: bfloat16 [20480, 1024], P(('gx', 'gy')), may hold values from -0.1875 to 0.1875
- box_down: bfloat16 [32768, 640], P(('gx', 'gy')), may hold values from -0.25 to 0.25
- up_one: bfloat16 [8192, 768], P(('gx', 'gy')), may hold values from -0.1875 to 0.1875
- down_one: bfloat16 [8192, 768], P(('gx', 'gy')), may hold values from -0.21875 to 0.21875
- up_two: bfloat16 [4096, 1536], P(('gx', 'gy')), may hold values from -0.125 to 0.125
- down_two: bfloat16 [4096, 1536], P(('gx', 'gy')), may hold values from -0.15625 to 0.15625
- up_root: bfloat16 [2048, 256], P(('gx', 'gy')), may hold values from -0.125 to 0.125
- down_root: bfloat16 [2048, 256], P(('gx', 'gy')), may hold values from -0.375 to 0.375
Outputs:
- solution: float32 [16, 512, 256], P(None, ('gx', 'gy'))
The draws below stay inside these ranges and needn't reach their ends.
All inputs are finite; a program needn't handle non-finite values.
Results may differ from the reference program's by a relative error of at most 0.014.
Values may be sent and summed in bfloat16 or wider, within the bound.
No kernel may reach another device: no remote copies, remote signals or barrier semaphores. Data moves between devices by JAX's collectives and lax.ppermute only.
A program may use at most 64 MiB of HBM per device.

```python
import jax
import jax.numpy as jnp
from jax import lax

R = 16
Q = 256
EDGE = 64
LEAF = 16
K0 = 256
I0 = 384
Z0 = 640
K1 = 512
Z1 = 768
K2 = 1024
Z2 = 1536
NROOT = 2
IR = 256
NLEAF = 512
N_GX = 4
N_GY = 8


def block_scale(key, extent, shards, low, top_value):
    gain = 1.0
    for position, shards_of in shards:
        draws = jax.random.uniform(jax.random.fold_in(jax.random.fold_in(key, 6), position), (shards_of,), jnp.float32, low / len(shards), top_value / len(shards))
        gain = gain * jnp.repeat(jnp.exp(draws), extent[position] // shards_of).reshape((-1,) + (1,) * (len(extent) - 1 - position))
    return gain


def scatter_about(key, dims, deviation, most, cuts=(), kind=jnp.bfloat16):
    array = jax.random.normal(key, dims, jnp.float32) * deviation
    if len(cuts) > 0:
        array = block_scale(key, dims, cuts, -0.22, 0.18) * array
    return jnp.clip(array, min=-most, max=most).astype(kind)


def setup_inputs(seed: int = 0) -> dict:
    streams_of = jax.random.split(jax.random.key(seed), 13)
    source = scatter_about(streams_of[0], (R, NLEAF, Q), 1.0, 6.0, ((1, 32),))
    leaf_flux = scatter_about(streams_of[1], (NLEAF * EDGE, Q), Q ** -0.5, 0.375, ((0, 32),))
    leaf_particular = scatter_about(streams_of[2], (NLEAF * Q, Q), Q ** -0.5, 0.375, ((0, 32),))
    leaf_lift = scatter_about(streams_of[3], (NLEAF * EDGE, Q), EDGE ** -0.5, 0.75, ((0, 32),))
    box_up = scatter_about(streams_of[4], (N_GX * N_GY * Z0, LEAF * EDGE), (LEAF * EDGE) ** -0.5, 0.1875, ((0, 32),))
    box_down = scatter_about(streams_of[5], (N_GX * N_GY * LEAF * EDGE, Z0), Z0 ** -0.5, 0.25, ((0, 32),))
    up_one = scatter_about(streams_of[6], (N_GX * N_GY * K0, Z1), (4 * K0) ** -0.5, 0.1875, ((0, 32),))
    down_one = scatter_about(streams_of[7], (N_GX * N_GY * K0, Z1), Z1 ** -0.5, 0.21875, ((0, 32),))
    up_two = scatter_about(streams_of[8], (N_GX * N_GY * K1 // 4, Z2), (4 * K1) ** -0.5, 0.125, ((0, 32),))
    down_two = scatter_about(streams_of[9], (N_GX * N_GY * K1 // 4, Z2), Z2 ** -0.5, 0.15625, ((0, 32),))
    up_root = scatter_about(streams_of[10], (N_GX * N_GY * K2 // 16, IR), (NROOT * K2) ** -0.5, 0.125, ((0, 32),))
    down_root = scatter_about(streams_of[11], (N_GX * N_GY * K2 // 16, IR), IR ** -0.5, 0.375, ((0, 32),))
    return dict(source=source, leaf_flux=leaf_flux, leaf_particular=leaf_particular, leaf_lift=leaf_lift, box_up=box_up, box_down=box_down, up_one=up_one, down_one=down_one, up_two=up_two, down_two=down_two, up_root=up_root, down_root=down_root)


def batched(form, left, right):
    return jnp.einsum(form, left.astype(jnp.float32), right.astype(jnp.float32), precision=lax.Precision.HIGHEST)


def reference(source, leaf_flux, leaf_particular, leaf_lift, box_up, box_down, up_one, down_one, up_two, down_two, up_root, down_root):
    count = N_GX * N_GY
    sources = source.reshape(R, count, LEAF, Q)
    flux = batched("rdlq,dleq->drle", sources, leaf_flux.reshape(count, LEAF, EDGE, Q))
    flux = flux.astype(jnp.bfloat16).reshape(count, R, LEAF * EDGE)
    box_state = batched("drk,dzk->drz", flux, box_up.reshape(count, Z0, LEAF * EDGE)).astype(jnp.bfloat16)
    first_terms = batched("drk,dkz->drz", box_state[:, :, I0:], up_one.reshape(count, K0, Z1))
    first_state = jnp.sum(first_terms.reshape(count // 4, 4, R, Z1), axis=1).astype(jnp.bfloat16)
    second_terms = batched("crk,ckz->crz", first_state[:, :, K0:], up_two.reshape(count // 4, K1, Z2))
    second_state = jnp.sum(second_terms.reshape(count // 16, 4, R, Z2), axis=1).astype(jnp.bfloat16)
    root_state = batched("crk,cki->ri", second_state[:, :, K1:], up_root.reshape(count // 16, K2, IR)).astype(jnp.bfloat16)
    top_bound = batched("ri,cki->crk", root_state, down_root.reshape(count // 16, K2, IR)).astype(jnp.bfloat16)
    second_input = jnp.concatenate([second_state[:, :, :K1], top_bound], axis=2)
    mid_bound = batched("prz,pckz->pcrk", second_input, down_two.reshape(count // 16, 4, K1, Z2))
    mid_bound = mid_bound.astype(jnp.bfloat16).reshape(count // 4, R, K1)
    first_input = jnp.concatenate([first_state[:, :, :K0], mid_bound], axis=2)
    box_bound = batched("prz,pckz->pcrk", first_input, down_one.reshape(count // 4, 4, K0, Z1))
    box_bound = box_bound.astype(jnp.bfloat16).reshape(count, R, K0)
    box_input = jnp.concatenate([box_state[:, :, :I0], box_bound], axis=2)
    leaf_bound = batched("drz,dkz->drk", box_input, box_down.reshape(count, LEAF * EDGE, Z0))
    leaf_bound = leaf_bound.astype(jnp.bfloat16).reshape(count, R, LEAF, EDGE)
    lifted = batched("drle,dleq->rdlq", leaf_bound, leaf_lift.reshape(count, LEAF, EDGE, Q))
    particular = batched("rdlq,dlqp->rdlp", sources, leaf_particular.reshape(count, LEAF, Q, Q))
    return (lifted + particular).reshape(R, count * LEAF, Q)
```

```python
import jax
import jax.numpy as jnp
from jax import lax
from jax.sharding import PartitionSpec as P

AXES = ("gx", "gy")


def contract(left, right):
    return lax.dot_general(
        left, right, (((1,), (1,)), ((), ())), preferred_element_type=jnp.float32
    )


def groups_of(size):
    count = lax.axis_size(AXES)
    return [list(range(start, start + size)) for start in range(0, count, size)]


def swap(pieces, size):
    return lax.all_to_all(pieces, AXES, 0, 0, axis_index_groups=groups_of(size))


def per_device(
    source,
    leaf_flux,
    leaf_particular,
    leaf_lift,
    box_up,
    box_down,
    up_one,
    down_one,
    up_two,
    down_two,
    up_root,
    down_root,
):
    rhs_count, leaves, points = source.shape
    edge_count = leaf_flux.shape[0] // leaves
    count = lax.axis_size(AXES)
    k_zero = up_one.shape[0]
    inner_dev = box_up.shape[0] - k_zero
    second_width = up_two.shape[0]
    first_inner = k_zero
    quad = (up_one.shape[1] - first_inner) // second_width
    k_one = up_one.shape[1] - first_inner
    root_width = up_root.shape[0]
    family = (up_two.shape[1] - k_one) // root_width

    root_up_all = lax.all_gather(
        up_root, AXES, axis_index_groups=groups_of(family), tiled=True
    )
    root_down_all = lax.all_gather(
        down_root, AXES, axis_index_groups=groups_of(family), tiled=True
    )

    flux = jnp.einsum(
        "rlq,leq->rle",
        source,
        leaf_flux.reshape(leaves, edge_count, points),
        preferred_element_type=jnp.float32,
    )
    flux = flux.astype(jnp.bfloat16).reshape(rhs_count, leaves * edge_count)
    box_state = contract(flux, box_up).astype(jnp.bfloat16)
    first_term = jnp.dot(box_state[:, inner_dev:], up_one, preferred_element_type=jnp.float32)
    first_term = first_term.astype(jnp.bfloat16)
    outer = first_term[:, first_inner:].reshape(rhs_count, quad, second_width).swapaxes(0, 1)
    inner = jnp.broadcast_to(first_term[:, :first_inner], (quad, rhs_count, first_inner))
    got = swap(jnp.concatenate([outer, inner], axis=2), quad)
    first_sum = jnp.sum(got.astype(jnp.float32), axis=0).astype(jnp.bfloat16)
    second_piece = first_sum[:, :second_width]
    first_inner_state = first_sum[:, second_width:]

    up_short = jnp.dot(
        up_two[:, k_one:], root_up_all, preferred_element_type=jnp.float32
    ).astype(jnp.bfloat16)
    down_short = jnp.dot(
        down_two[:, k_one:], root_down_all, preferred_element_type=jnp.float32
    ).astype(jnp.bfloat16)

    second_term = jnp.dot(
        second_piece, jnp.concatenate([up_two[:, :k_one], up_short], axis=1),
        preferred_element_type=jnp.float32,
    ).astype(jnp.bfloat16)
    rows = rhs_count // family
    got = swap(second_term.reshape(family, rows, second_term.shape[1]), family)
    second_rows = jnp.sum(got.astype(jnp.float32), axis=0)
    second_all = lax.all_to_all(
        jnp.broadcast_to(second_rows, (count,) + second_rows.shape), AXES, 0, 0
    ).reshape(count // family, rhs_count, second_rows.shape[1])
    own = lax.axis_index(AXES) // family
    root_state = jnp.sum(second_all[:, :, k_one:], axis=0).astype(jnp.bfloat16)
    second_inner = lax.dynamic_index_in_dim(
        second_all[:, :, :k_one], own, 0, keepdims=False
    ).astype(jnp.bfloat16)
    mid_piece = contract(
        jnp.concatenate([second_inner, root_state], axis=1),
        jnp.concatenate([down_two[:, :k_one], down_short], axis=1),
    ).astype(jnp.bfloat16)
    mid_bound = swap(jnp.broadcast_to(mid_piece, (quad,) + mid_piece.shape), quad)
    mid_bound = mid_bound.swapaxes(0, 1).reshape(rhs_count, k_one)
    first_input = jnp.concatenate([first_inner_state, mid_bound], axis=1)
    box_bound = contract(first_input, down_one).astype(jnp.bfloat16)
    box_input = jnp.concatenate([box_state[:, :inner_dev], box_bound], axis=1)
    leaf_bound = (
        contract(box_input, box_down).astype(jnp.bfloat16).reshape(rhs_count, leaves, edge_count)
    )
    lifted = jnp.einsum(
        "rle,leq->rlq",
        leaf_bound,
        leaf_lift.reshape(leaves, edge_count, points),
        preferred_element_type=jnp.float32,
    )
    particular = jnp.einsum(
        "rlq,lqp->rlp",
        source,
        leaf_particular.reshape(leaves, points, points),
        preferred_element_type=jnp.float32,
    )
    return lifted + particular


def solution(mesh):
    return jax.shard_map(
        per_device,
        mesh=mesh,
        in_specs=(P(None, AXES, None),) + (P(AXES, None),) * 11,
        out_specs=P(None, AXES, None),
        check_vma=False,
    )
```

```python
import jax
import jax.numpy as jnp
from jax import lax
from jax.sharding import PartitionSpec as P

AXES = ("gx", "gy")


def contract(left, right):
    return lax.dot_general(
        left, right, (((1,), (1,)), ((), ())), preferred_element_type=jnp.float32
    )


def product(left, right):
    return jnp.dot(left, right, preferred_element_type=jnp.float32)


def partner_sum(term, bit):
    count = lax.axis_size(AXES)
    other = lax.ppermute(term.astype(jnp.bfloat16), AXES, [(i, i ^ bit) for i in range(count)])
    return term + other.astype(jnp.float32)


def gathered(block, size):
    count = lax.axis_size(AXES)
    groups = [list(range(start, start + size)) for start in range(0, count, size)]
    return lax.all_gather(block, AXES, axis_index_groups=groups, tiled=True)


def per_device(
    source,
    leaf_flux,
    leaf_particular,
    leaf_lift,
    box_up,
    box_down,
    up_one,
    down_one,
    up_two,
    down_two,
    up_root,
    down_root,
):
    rhs_count, leaves, points = source.shape
    edge_count = leaf_flux.shape[0] // leaves
    count = lax.axis_size(AXES)
    k_zero = up_one.shape[0]
    inner_dev = box_up.shape[0] - k_zero
    k_one = up_one.shape[1] - k_zero
    quad = k_one // up_two.shape[0]
    family = (up_two.shape[1] - k_one) // up_root.shape[0]
    root_points = up_root.shape[1]

    up_two_box = gathered(up_two, quad)
    roots = gathered(jnp.concatenate([up_root, down_root], axis=1), family)
    down_two_box = gathered(down_two, quad)

    flux = jnp.einsum(
        "rlq,leq->rle",
        source,
        leaf_flux.reshape(leaves, edge_count, points),
        preferred_element_type=jnp.float32,
    )
    flux = flux.astype(jnp.bfloat16).reshape(rhs_count, leaves * edge_count)
    box_state = contract(flux, box_up).astype(jnp.bfloat16)
    first_sum = product(box_state[:, inner_dev:], up_one)
    bit = 1
    while bit < quad:
        first_sum = partner_sum(first_sum, bit)
        bit *= 2
    first_state = first_sum.astype(jnp.bfloat16)

    second_term = product(first_state[:, k_zero:], up_two_box)
    root_term = product(second_term[:, k_one:].astype(jnp.bfloat16), roots[:, :root_points])
    total = jnp.concatenate([second_term[:, :k_one], root_term], axis=1)
    while bit < family:
        total = partner_sum(total, bit)
        bit *= 2
    second_inner = total[:, :k_one].astype(jnp.bfloat16)
    root_sum = total[:, k_one:]
    while bit < count:
        root_sum = partner_sum(root_sum, bit)
        bit *= 2
    root_state = root_sum.astype(jnp.bfloat16)

    top_bound = contract(root_state, roots[:, root_points:]).astype(jnp.bfloat16)
    second_input = jnp.concatenate([second_inner, top_bound], axis=1)
    mid_bound = contract(second_input, down_two_box).astype(jnp.bfloat16)
    first_input = jnp.concatenate([first_state[:, :k_zero], mid_bound], axis=1)
    box_bound = contract(first_input, down_one).astype(jnp.bfloat16)
    box_input = jnp.concatenate([box_state[:, :inner_dev], box_bound], axis=1)
    leaf_bound = (
        contract(box_input, box_down).astype(jnp.bfloat16).reshape(rhs_count, leaves, edge_count)
    )
    lifted = jnp.einsum(
        "rle,leq->rlq",
        leaf_bound,
        leaf_lift.reshape(leaves, edge_count, points),
        preferred_element_type=jnp.float32,
    )
    particular = jnp.einsum(
        "rlq,lqp->rlp",
        source,
        leaf_particular.reshape(leaves, points, points),
        preferred_element_type=jnp.float32,
    )
    return lifted + particular


def solution(mesh):
    return jax.shard_map(
        per_device,
        mesh=mesh,
        in_specs=(P(None, AXES, None),) + (P(AXES, None),) * 11,
        out_specs=P(None, AXES, None),
        check_vma=False,
    )
```

```python
import jax
import jax.numpy as jnp
from jax import lax
from jax.sharding import PartitionSpec as P

AXES = ("gx", "gy")


def contract(left, right):
    return lax.dot_general(
        left, right, (((1,), (1,)), ((), ())), preferred_element_type=jnp.float32
    )


def product(left, right):
    return jnp.dot(left, right, preferred_element_type=jnp.float32)


def rounded(value):
    return value.astype(jnp.bfloat16)


def swap(value, bit, pair, upper):
    count = lax.axis_size(AXES)
    return lax.ppermute(
        value, AXES, [(i, i ^ bit) for i in range(count) if bool(i & pair) == upper]
    )


def lift(value, pair):
    count = lax.axis_size(AXES)
    return lax.ppermute(value, AXES, [(i, i ^ pair) for i in range(count) if not i & pair])


def drop(value, pair):
    count = lax.axis_size(AXES)
    return lax.ppermute(value, AXES, [(i, i ^ pair) for i in range(count) if i & pair])


def bits_of(first, last):
    bits = []
    while first < last:
        bits.append(first)
        first *= 2
    return bits


def place_pair(joined, other, high, axis):
    return jnp.concatenate(
        [jnp.where(high, other, joined), jnp.where(high, joined, other)], axis=axis
    )


def family_rows(block, pair, place):
    joined = jnp.stack([block, drop(block, pair)])
    axis = 1
    for bit in reversed(bits_of(1, pair)):
        other = swap(joined, bit, pair, False)
        high = place & bit != 0
        joined = jnp.stack(
            [jnp.where(high, other, joined), jnp.where(high, joined, other)], axis=axis
        )
        axis += 1
    return lift(joined.reshape(-1, block.shape[1]), pair)


def per_device(
    source,
    leaf_flux,
    leaf_particular,
    leaf_lift,
    box_up,
    box_down,
    up_one,
    down_one,
    up_two,
    down_two,
    up_root,
    down_root,
):
    rhs_count, leaves, points = source.shape
    edge_count = leaf_flux.shape[0] // leaves
    count = lax.axis_size(AXES)
    place = lax.axis_index(AXES)
    k_zero = up_one.shape[0]
    inner_dev = box_up.shape[0] - k_zero
    k_one = up_one.shape[1] - k_zero
    width = up_two.shape[0]
    quad = k_one // width
    family = (up_two.shape[1] - k_one) // up_root.shape[0]
    pair = family // 2
    upper = place & pair != 0

    up_two_low = lift(up_two, pair)
    down_two_low = lift(down_two, pair)
    up_root_all = family_rows(up_root, pair, place)
    down_root_all = family_rows(down_root, pair, place)

    flux = jnp.einsum(
        "rlq,leq->rle",
        source,
        leaf_flux.reshape(leaves, edge_count, points),
        preferred_element_type=jnp.float32,
    )
    flux = rounded(flux).reshape(rhs_count, leaves * edge_count)
    box_state = rounded(contract(flux, box_up))
    first_term = product(box_state[:, inner_dev:], up_one)
    first_low = lift(rounded(first_term), pair).astype(jnp.float32)
    first_sum = jnp.concatenate([first_low, first_term], axis=0)
    for bit in bits_of(1, quad):
        first_sum = first_sum + swap(rounded(first_sum), bit, pair, True).astype(jnp.float32)
    first_state = rounded(first_sum)

    piece = lax.dynamic_slice_in_dim(first_state, k_zero + place % quad * width, width, 1)
    second_sum = product(piece[:rhs_count], up_two_low) + product(piece[rhs_count:], up_two)
    for bit in bits_of(1, pair):
        second_sum = second_sum + swap(rounded(second_sum), bit, pair, True).astype(jnp.float32)
    second_state = rounded(second_sum)

    root_sum = product(second_state[:, k_one:], up_root_all)
    for bit in bits_of(family, count):
        root_sum = root_sum + swap(rounded(root_sum), bit, pair, True).astype(jnp.float32)
    root_state = rounded(root_sum)

    top_bound = rounded(contract(root_state, down_root_all))
    second_input = jnp.concatenate([second_state[:, :k_one], top_bound], axis=1)
    mid_bound = rounded(
        jnp.concatenate(
            [contract(second_input, down_two_low), contract(second_input, down_two)], axis=0
        )
    )
    for bit in bits_of(1, quad):
        mid_bound = place_pair(mid_bound, swap(mid_bound, bit, pair, True), place & bit != 0, 1)
    both = jnp.concatenate([first_state[:, :k_zero], mid_bound], axis=1)
    first_input = jnp.where(upper, both[rhs_count:], drop(both[:rhs_count], pair))

    box_bound = rounded(contract(first_input, down_one))
    box_input = jnp.concatenate([box_state[:, :inner_dev], box_bound], axis=1)
    leaf_bound = rounded(contract(box_input, box_down)).reshape(rhs_count, leaves, edge_count)
    lifted = jnp.einsum(
        "rle,leq->rlq",
        leaf_bound,
        leaf_lift.reshape(leaves, edge_count, points),
        preferred_element_type=jnp.float32,
    )
    particular = jnp.einsum(
        "rlq,lqp->rlp",
        source,
        leaf_particular.reshape(leaves, points, points),
        preferred_element_type=jnp.float32,
    )
    return lifted + particular


def solution(mesh):
    return jax.shard_map(
        per_device,
        mesh=mesh,
        in_specs=(P(None, AXES, None),) + (P(AXES, None),) * 11,
        out_specs=P(None, AXES, None),
        check_vma=False,
    )
```

```python
import jax
import jax.numpy as jnp
from jax import lax
from jax.sharding import PartitionSpec as P

AXES = ("gx", "gy")


def contract(left, right):
    return lax.dot_general(
        left, right, (((1,), (1,)), ((), ())), preferred_element_type=jnp.float32
    )


def product(left, right):
    return jnp.dot(left, right, preferred_element_type=jnp.float32)


def rounded(value):
    return value.astype(jnp.bfloat16)


def swap(value, bit, pair, upper):
    count = lax.axis_size(AXES)
    return lax.ppermute(
        value, AXES, [(i, i ^ bit if bool(i & pair) == upper else i) for i in range(count)]
    )


def across(value, pair):
    count = lax.axis_size(AXES)
    return lax.ppermute(value, AXES, [(i, i ^ pair) for i in range(count)])


def bits_of(first, last):
    bits = []
    while first < last:
        bits.append(first)
        first *= 2
    return bits


def place_pair(joined, other, high, axis):
    return jnp.concatenate(
        [jnp.where(high, other, joined), jnp.where(high, joined, other)], axis=axis
    )


def family_rows(block, pair, place):
    joined = jnp.stack([block, across(block, pair)])
    axis = 1
    for bit in reversed(bits_of(1, pair)):
        other = swap(joined, bit, pair, False)
        high = place & bit != 0
        joined = jnp.stack(
            [jnp.where(high, other, joined), jnp.where(high, joined, other)], axis=axis
        )
        axis += 1
    return across(joined.reshape(-1, block.shape[1]), pair)


def per_device(
    source,
    leaf_flux,
    leaf_particular,
    leaf_lift,
    box_up,
    box_down,
    up_one,
    down_one,
    up_two,
    down_two,
    up_root,
    down_root,
):
    rhs_count, leaves, points = source.shape
    edge_count = leaf_flux.shape[0] // leaves
    count = lax.axis_size(AXES)
    place = lax.axis_index(AXES)
    k_zero = up_one.shape[0]
    inner_dev = box_up.shape[0] - k_zero
    k_one = up_one.shape[1] - k_zero
    width = up_two.shape[0]
    quad = k_one // width
    family = (up_two.shape[1] - k_one) // up_root.shape[0]
    pair = family // 2
    upper = place & pair != 0

    up_two_low = across(up_two, pair)
    down_two_low = across(down_two, pair)
    up_root_all = family_rows(up_root, pair, place)
    down_root_all = family_rows(down_root, pair, place)

    flux = jnp.einsum(
        "rlq,leq->rle",
        source,
        leaf_flux.reshape(leaves, edge_count, points),
        preferred_element_type=jnp.float32,
    )
    flux = rounded(flux).reshape(rhs_count, leaves * edge_count)
    box_state = rounded(contract(flux, box_up))
    first_term = product(box_state[:, inner_dev:], up_one)
    first_low = across(rounded(first_term), pair).astype(jnp.float32)
    first_sum = jnp.concatenate([first_low, first_term], axis=0)
    for bit in bits_of(1, quad):
        first_sum = first_sum + swap(rounded(first_sum), bit, pair, True).astype(jnp.float32)
    first_state = rounded(first_sum)

    piece = lax.dynamic_slice_in_dim(first_state, k_zero + place % quad * width, width, 1)
    second_sum = product(piece[:rhs_count], up_two_low) + product(piece[rhs_count:], up_two)
    for bit in bits_of(1, pair):
        second_sum = second_sum + swap(rounded(second_sum), bit, pair, True).astype(jnp.float32)
    second_state = rounded(second_sum)

    root_sum = product(second_state[:, k_one:], up_root_all)
    for bit in bits_of(family, count):
        root_sum = root_sum + swap(rounded(root_sum), bit, pair, True).astype(jnp.float32)
    root_state = rounded(root_sum)

    top_bound = rounded(contract(root_state, down_root_all))
    second_input = jnp.concatenate([second_state[:, :k_one], top_bound], axis=1)
    mid_bound = rounded(
        jnp.concatenate(
            [contract(second_input, down_two_low), contract(second_input, down_two)], axis=0
        )
    )
    for bit in bits_of(1, quad):
        mid_bound = place_pair(mid_bound, swap(mid_bound, bit, pair, True), place & bit != 0, 1)
    both = jnp.concatenate([first_state[:, :k_zero], mid_bound], axis=1)
    first_input = jnp.where(upper, both[rhs_count:], across(both[:rhs_count], pair))

    box_bound = rounded(contract(first_input, down_one))
    box_input = jnp.concatenate([box_state[:, :inner_dev], box_bound], axis=1)
    leaf_bound = rounded(contract(box_input, box_down)).reshape(rhs_count, leaves, edge_count)
    lifted = jnp.einsum(
        "rle,leq->rlq",
        leaf_bound,
        leaf_lift.reshape(leaves, edge_count, points),
        preferred_element_type=jnp.float32,
    )
    particular = jnp.einsum(
        "rlq,lqp->rlp",
        source,
        leaf_particular.reshape(leaves, points, points),
        preferred_element_type=jnp.float32,
    )
    return lifted + particular


def solution(mesh):
    return jax.shard_map(
        per_device,
        mesh=mesh,
        in_specs=(P(None, AXES, None),) + (P(AXES, None),) * 11,
        out_specs=P(None, AXES, None),
        check_vma=False,
    )
```

```python
import jax
import jax.numpy as jnp
from jax import lax
from jax.sharding import PartitionSpec as P

AXES = ("gx", "gy")


def contract(left, right):
    return lax.dot_general(
        left, right, (((1,), (1,)), ((), ())), preferred_element_type=jnp.float32
    )


def product(left, right):
    return jnp.dot(left, right, preferred_element_type=jnp.float32)


def rounded(value):
    return value.astype(jnp.bfloat16)


def swap(value, mask):
    count = lax.axis_size(AXES)
    return lax.ppermute(value, AXES, [(i, i ^ mask) for i in range(count)])


def partner_sum(total, mask):
    return total + swap(rounded(total), mask).astype(jnp.float32)


def bits_of(first, last):
    bits = []
    while first < last:
        bits.append(first)
        first *= 2
    return bits


def placed(pieces, place, axis):
    bit = len(pieces) // 2
    if bit == 0:
        return pieces[0]
    low, high = placed(pieces[:bit], place, axis), placed(pieces[bit:], place, axis)
    upper = place & bit != 0
    return jnp.concatenate(
        [jnp.where(upper, high, low), jnp.where(upper, low, high)], axis=axis
    )


def family_rows(block, family, place):
    joined = block
    axis = 0
    shape = block.shape
    joined = joined[None]
    bits = bits_of(1, family)
    done = []
    for bit in bits[-2::-1] + bits[-1:]:
        other = swap(joined, bit)
        upper = place & bit != 0
        axis = sum(1 for d in done if d > bit)
        joined = jnp.stack(
            [jnp.where(upper, other, joined), jnp.where(upper, joined, other)], axis=axis
        )
        done.append(bit)
    return joined.reshape(-1, shape[1])


def per_device(
    source,
    leaf_flux,
    leaf_particular,
    leaf_lift,
    box_up,
    box_down,
    up_one,
    down_one,
    up_two,
    down_two,
    up_root,
    down_root,
):
    rhs_count, leaves, points = source.shape
    edge_count = leaf_flux.shape[0] // leaves
    count = lax.axis_size(AXES)
    place = lax.axis_index(AXES)
    k_zero = up_one.shape[0]
    inner_dev = box_up.shape[0] - k_zero
    k_one = up_one.shape[1] - k_zero
    width = up_two.shape[0]
    quad = k_one // width
    family = (up_two.shape[1] - k_one) // up_root.shape[0]
    near = quad // 2
    root_points = up_root.shape[1]

    up_two_near = swap(up_two, near)
    down_two_all = [down_two] + [swap(down_two, mask) for mask in range(1, quad)]
    roots = family_rows(jnp.concatenate([up_root, down_root], axis=1), family, place)

    flux = jnp.einsum(
        "rlq,leq->rle",
        source,
        leaf_flux.reshape(leaves, edge_count, points),
        preferred_element_type=jnp.float32,
    )
    flux = rounded(flux).reshape(rhs_count, leaves * edge_count)
    box_state = rounded(contract(flux, box_up))
    first_sum = product(box_state[:, inner_dev:], up_one)
    for bit in bits_of(1, quad):
        first_sum = partner_sum(first_sum, bit)
    first_state = rounded(first_sum)

    def piece(mask):
        start = k_zero + (place ^ mask) % quad * width
        return lax.dynamic_slice_in_dim(first_state, start, width, 1)

    second_sum = product(piece(0), up_two) + product(piece(near), up_two_near)
    for bit in bits_of(1, family):
        if bit != near:
            second_sum = partner_sum(second_sum, bit)
    second_state = rounded(second_sum)

    root_sum = product(second_state[:, k_one:], roots[:, :root_points])
    for bit in bits_of(family, count):
        root_sum = partner_sum(root_sum, bit)
    root_state = rounded(root_sum)

    top_bound = rounded(contract(root_state, roots[:, root_points:]))
    second_input = jnp.concatenate([second_state[:, :k_one], top_bound], axis=1)
    mid_bound = placed([rounded(contract(second_input, part)) for part in down_two_all], place, 1)
    first_input = jnp.concatenate([first_state[:, :k_zero], mid_bound], axis=1)

    box_bound = rounded(contract(first_input, down_one))
    box_input = jnp.concatenate([box_state[:, :inner_dev], box_bound], axis=1)
    leaf_bound = rounded(contract(box_input, box_down)).reshape(rhs_count, leaves, edge_count)
    lifted = jnp.einsum(
        "rle,leq->rlq",
        leaf_bound,
        leaf_lift.reshape(leaves, edge_count, points),
        preferred_element_type=jnp.float32,
    )
    particular = jnp.einsum(
        "rlq,lqp->rlp",
        source,
        leaf_particular.reshape(leaves, points, points),
        preferred_element_type=jnp.float32,
    )
    return lifted + particular


def solution(mesh):
    return jax.shard_map(
        per_device,
        mesh=mesh,
        in_specs=(P(None, AXES, None),) + (P(AXES, None),) * 11,
        out_specs=P(None, AXES, None),
        check_vma=False,
    )
```

```python
import jax
import jax.numpy as jnp
from jax import lax
from jax.sharding import PartitionSpec as P

AXES = ("gx", "gy")


def contract(left, right):
    return lax.dot_general(
        left, right, (((1,), (1,)), ((), ())), preferred_element_type=jnp.float32
    )


def product(left, right):
    return jnp.dot(left, right, preferred_element_type=jnp.float32)


def rounded(value):
    return value.astype(jnp.bfloat16)


def swap(value, mask):
    count = lax.axis_size(AXES)
    return lax.ppermute(value, AXES, [(i, i ^ mask) for i in range(count)])


def partner_sum(total, mask):
    return total + swap(rounded(total), mask).astype(jnp.float32)


def bits_of(first, last):
    bits = []
    while first < last:
        bits.append(first)
        first *= 2
    return bits


def placed(pieces, place, axis):
    bit = len(pieces) // 2
    if bit == 0:
        return pieces[0]
    low, high = placed(pieces[:bit], place, axis), placed(pieces[bit:], place, axis)
    upper = place & bit != 0
    return jnp.concatenate(
        [jnp.where(upper, high, low), jnp.where(upper, low, high)], axis=axis
    )


def joined_pair(joined, other, upper, axis):
    return jnp.stack(
        [jnp.where(upper, other, joined), jnp.where(upper, joined, other)], axis=axis
    )


def tie(*values):
    return lax.optimization_barrier(values)


def quad_order(halves, width, place):
    own, other = halves
    upper = place & 1 != 0
    blocks = []
    for start in range(0, own.shape[1], width):
        left, right = own[:, start : start + width], other[:, start : start + width]
        blocks += [jnp.where(upper, right, left), jnp.where(upper, left, right)]
    return jnp.concatenate(blocks, axis=1)


def per_device(
    source,
    leaf_flux,
    leaf_particular,
    leaf_lift,
    box_up,
    box_down,
    up_one,
    down_one,
    up_two,
    down_two,
    up_root,
    down_root,
):
    rhs_count, leaves, points = source.shape
    edge_count = leaf_flux.shape[0] // leaves
    count = lax.axis_size(AXES)
    place = lax.axis_index(AXES)
    k_zero = up_one.shape[0]
    inner_dev = box_up.shape[0] - k_zero
    k_one = up_one.shape[1] - k_zero
    width = up_two.shape[0]
    quad = k_one // width
    family = (up_two.shape[1] - k_one) // up_root.shape[0]
    near = quad // 2
    pair = family // 2
    root_points = up_root.shape[1]

    far = pair // 2

    roots = jnp.concatenate([up_root, down_root], axis=1)
    roots_far = swap(roots, far)
    up_two_near = swap(up_two, near)

    flux = jnp.einsum(
        "rlq,leq->rle",
        source,
        leaf_flux.reshape(leaves, edge_count, points),
        preferred_element_type=jnp.float32,
    )
    flux = rounded(flux).reshape(rhs_count, leaves * edge_count)
    box_state = rounded(contract(flux, box_up))
    first_sum = product(box_state[:, inner_dev:], up_one)

    first_sum, roots_far = tie(first_sum, roots_far)
    roots = joined_pair(roots, roots_far, place & far != 0, 0)
    roots_near = swap(roots, near)
    first_sum = partner_sum(first_sum, 1)

    first_sum, roots_near = tie(first_sum, roots_near)
    roots = joined_pair(roots, roots_near, place & near != 0, 1)
    roots_one = swap(roots, 1)
    first_sum = partner_sum(first_sum, near)
    first_state = rounded(first_sum)

    def piece(mask):
        start = k_zero + (place ^ mask) % quad * width
        return lax.dynamic_slice_in_dim(first_state, start, width, 1)

    second_sum = product(piece(0), up_two) + product(piece(near), up_two_near)
    second_sum, roots_one = tie(second_sum, roots_one)
    roots = joined_pair(roots, roots_one, place & 1 != 0, 2)
    roots_pair = swap(roots, pair)
    down_two_near = swap(down_two, near)
    second_sum = partner_sum(second_sum, far)

    second_sum, roots_pair = tie(second_sum, roots_pair)
    roots = joined_pair(roots, roots_pair, place & pair != 0, 0)
    roots = roots.reshape(-1, roots.shape[-1])
    second_sum = partner_sum(second_sum, 1)
    second_sum = partner_sum(second_sum, pair)
    second_state = rounded(second_sum)

    root_sum = product(second_state[:, k_one:], roots[:, :root_points])
    root_sum, down_two_near = tie(root_sum, down_two_near)
    for bit in bits_of(family, count):
        root_sum = partner_sum(root_sum, bit)
    root_state = rounded(root_sum)

    top_bound = rounded(contract(root_state, roots[:, root_points:]))
    second_input = jnp.concatenate([second_state[:, :k_one], top_bound], axis=1)
    own_mid = rounded(contract(second_input, down_two))
    near_mid = rounded(contract(second_input, down_two_near))
    mid_bound = placed([own_mid, near_mid], place // near, 1)
    other_mid = swap(mid_bound, 1)
    mid_bound = quad_order((mid_bound, other_mid), width, place)
    first_input = jnp.concatenate([first_state[:, :k_zero], mid_bound], axis=1)

    box_bound = rounded(contract(first_input, down_one))
    box_input = jnp.concatenate([box_state[:, :inner_dev], box_bound], axis=1)
    leaf_bound = rounded(contract(box_input, box_down)).reshape(rhs_count, leaves, edge_count)
    lifted = jnp.einsum(
        "rle,leq->rlq",
        leaf_bound,
        leaf_lift.reshape(leaves, edge_count, points),
        preferred_element_type=jnp.float32,
    )
    particular = jnp.einsum(
        "rlq,lqp->rlp",
        source,
        leaf_particular.reshape(leaves, points, points),
        preferred_element_type=jnp.float32,
    )
    return lifted + particular


def solution(mesh):
    return jax.shard_map(
        per_device,
        mesh=mesh,
        in_specs=(P(None, AXES, None),) + (P(AXES, None),) * 11,
        out_specs=P(None, AXES, None),
        check_vma=False,
    )
```

```python
import jax
import jax.numpy as jnp
from jax import lax
from jax.sharding import PartitionSpec as P

AXES = ("gx", "gy")


def contract(left, right):
    return lax.dot_general(
        left, right, (((1,), (1,)), ((), ())), preferred_element_type=jnp.float32
    )


def product(left, right):
    return jnp.dot(left, right, preferred_element_type=jnp.float32)


def rounded(value):
    return value.astype(jnp.bfloat16)


def swap(value, mask):
    count = lax.axis_size(AXES)
    return lax.ppermute(value, AXES, [(i, i ^ mask) for i in range(count)])


def partner_sum(total, mask):
    return total + swap(rounded(total), mask).astype(jnp.float32)


def bits_of(first, last):
    bits = []
    while first < last:
        bits.append(first)
        first *= 2
    return bits


def placed(pieces, place, axis):
    bit = len(pieces) // 2
    if bit == 0:
        return pieces[0]
    low, high = placed(pieces[:bit], place, axis), placed(pieces[bit:], place, axis)
    upper = place & bit != 0
    return jnp.concatenate(
        [jnp.where(upper, high, low), jnp.where(upper, low, high)], axis=axis
    )


def joined_pair(joined, other, upper, axis):
    return jnp.stack(
        [jnp.where(upper, other, joined), jnp.where(upper, joined, other)], axis=axis
    )


def tie(*values):
    return lax.optimization_barrier(values)


def per_device(
    source,
    leaf_flux,
    leaf_particular,
    leaf_lift,
    box_up,
    box_down,
    up_one,
    down_one,
    up_two,
    down_two,
    up_root,
    down_root,
):
    rhs_count, leaves, points = source.shape
    edge_count = leaf_flux.shape[0] // leaves
    count = lax.axis_size(AXES)
    place = lax.axis_index(AXES)
    k_zero = up_one.shape[0]
    inner_dev = box_up.shape[0] - k_zero
    k_one = up_one.shape[1] - k_zero
    width = up_two.shape[0]
    quad = k_one // width
    family = (up_two.shape[1] - k_one) // up_root.shape[0]
    near = quad // 2
    pair = family // 2
    root_points = up_root.shape[1]

    far = pair // 2

    flux = jnp.einsum(
        "rlq,leq->rle",
        source,
        leaf_flux.reshape(leaves, edge_count, points),
        preferred_element_type=jnp.float32,
    )
    flux = rounded(flux).reshape(rhs_count, leaves * edge_count)
    box_state = rounded(contract(flux, box_up))
    first_sum = product(box_state[:, inner_dev:], up_one)

    roots = jnp.concatenate([up_root, down_root], axis=1)
    roots_far = swap(roots, far)
    first_sum = partner_sum(first_sum, 1)

    first_sum, roots_far = tie(first_sum, roots_far)
    roots = joined_pair(roots, roots_far, place & far != 0, 0)
    roots_one = swap(roots, 1)
    first_sum = partner_sum(first_sum, near)
    first_state = rounded(first_sum)

    piece = lax.dynamic_slice_in_dim(first_state, k_zero + place % quad * width, width, 1)
    second_sum = product(piece, up_two)
    second_sum, roots_one = tie(second_sum, roots_one)
    roots = joined_pair(roots, roots_one, place & 1 != 0, 1)
    roots_near = swap(roots, near)
    second_sum = partner_sum(second_sum, far | pair)

    second_sum = partner_sum(second_sum, 1 | pair)
    second_sum, roots_near = tie(second_sum, roots_near)
    roots = joined_pair(roots, roots_near, place & near != 0, 1)
    roots_pair = swap(roots, pair)
    second_sum = partner_sum(second_sum, near | pair)
    second_sum = partner_sum(second_sum, pair)
    second_state = rounded(second_sum)
    roots = joined_pair(roots, roots_pair, place & pair != 0, 0)
    roots = roots.reshape(-1, roots.shape[-1])

    root_sum = product(second_state[:, k_one:], roots[:, :root_points])
    for bit in bits_of(family, count):
        root_sum = partner_sum(root_sum, bit | pair)
    root_state = rounded(root_sum)

    top_bound = rounded(contract(root_state, roots[:, root_points:]))
    second_input = jnp.concatenate([second_state[:, :k_one], top_bound], axis=1)
    mid_bound = rounded(contract(second_input, down_two))
    mid_bound = placed([mid_bound, swap(mid_bound, 1)], place, 1)
    mid_bound = placed([mid_bound, swap(mid_bound, near)], place // near, 1)
    first_input = jnp.concatenate([first_state[:, :k_zero], mid_bound], axis=1)

    box_bound = rounded(contract(first_input, down_one))
    box_input = jnp.concatenate([box_state[:, :inner_dev], box_bound], axis=1)
    leaf_bound = rounded(contract(box_input, box_down)).reshape(rhs_count, leaves, edge_count)
    lifted = jnp.einsum(
        "rle,leq->rlq",
        leaf_bound,
        leaf_lift.reshape(leaves, edge_count, points),
        preferred_element_type=jnp.float32,
    )
    particular = jnp.einsum(
        "rlq,lqp->rlp",
        source,
        leaf_particular.reshape(leaves, points, points),
        preferred_element_type=jnp.float32,
    )
    return lifted + particular


def solution(mesh):
    return jax.shard_map(
        per_device,
        mesh=mesh,
        in_specs=(P(None, AXES, None),) + (P(AXES, None),) * 11,
        out_specs=P(None, AXES, None),
        check_vma=False,
    )
```

```python
import jax
import jax.numpy as jnp
from jax import lax
from jax.sharding import PartitionSpec as P

AXES = ("gx", "gy")


def contract(left, right):
    return lax.dot_general(
        left, right, (((1,), (1,)), ((), ())), preferred_element_type=jnp.float32
    )


def product(left, right):
    return jnp.dot(left, right, preferred_element_type=jnp.float32)


def rounded(value):
    return value.astype(jnp.bfloat16)


def swap(value, mask):
    count = lax.axis_size(AXES)
    return lax.ppermute(value, AXES, [(i, i ^ mask) for i in range(count)])


def partner_sum(total, mask):
    return total + swap(rounded(total), mask).astype(jnp.float32)


def bits_of(first, last):
    bits = []
    while first < last:
        bits.append(first)
        first *= 2
    return bits


def placed(pieces, place, axis):
    bit = len(pieces) // 2
    if bit == 0:
        return pieces[0]
    low, high = placed(pieces[:bit], place, axis), placed(pieces[bit:], place, axis)
    upper = place & bit != 0
    return jnp.concatenate(
        [jnp.where(upper, high, low), jnp.where(upper, low, high)], axis=axis
    )


def joined_pair(joined, other, upper, axis):
    return jnp.stack(
        [jnp.where(upper, other, joined), jnp.where(upper, joined, other)], axis=axis
    )


def tie(*values):
    return lax.optimization_barrier(values)


def per_device(
    source,
    leaf_flux,
    leaf_particular,
    leaf_lift,
    box_up,
    box_down,
    up_one,
    down_one,
    up_two,
    down_two,
    up_root,
    down_root,
):
    rhs_count, leaves, points = source.shape
    edge_count = leaf_flux.shape[0] // leaves
    count = lax.axis_size(AXES)
    place = lax.axis_index(AXES)
    k_zero = up_one.shape[0]
    inner_dev = box_up.shape[0] - k_zero
    k_one = up_one.shape[1] - k_zero
    width = up_two.shape[0]
    quad = k_one // width
    family = (up_two.shape[1] - k_one) // up_root.shape[0]
    near = quad // 2
    pair = family // 2
    root_points = up_root.shape[1]

    far = pair // 2

    roots = jnp.concatenate([up_root, down_root], axis=1)
    roots = lax.all_to_all(
        jnp.broadcast_to(roots, (pair,) + roots.shape),
        AXES,
        0,
        0,
        axis_index_groups=[list(range(i, i + pair)) for i in range(0, count, pair)],
    )
    roots = joined_pair(roots, swap(roots, pair), place & pair != 0, 0)
    roots = roots.reshape(-1, roots.shape[-1])

    flux = jnp.einsum(
        "rlq,leq->rle",
        source,
        leaf_flux.reshape(leaves, edge_count, points),
        preferred_element_type=jnp.float32,
    )
    flux = rounded(flux).reshape(rhs_count, leaves * edge_count)
    box_state = rounded(contract(flux, box_up))
    first_sum = product(box_state[:, inner_dev:], up_one)

    for bit in bits_of(1, quad):
        first_sum = partner_sum(first_sum, bit)
    first_state = rounded(first_sum)

    piece = lax.dynamic_slice_in_dim(first_state, k_zero + place % quad * width, width, 1)
    second_sum = product(piece, up_two)
    for mask in (far | pair, 1 | pair, near | pair, pair):
        second_sum = partner_sum(second_sum, mask)
    second_state = rounded(second_sum)

    root_sum = product(second_state[:, k_one:], roots[:, :root_points])
    for bit in bits_of(family, count):
        root_sum = partner_sum(root_sum, bit | pair)
    root_state = rounded(root_sum)

    top_bound = rounded(contract(root_state, roots[:, root_points:]))
    second_input = jnp.concatenate([second_state[:, :k_one], top_bound], axis=1)
    mid_bound = rounded(contract(second_input, down_two))
    mid_bound = placed([mid_bound, swap(mid_bound, 1)], place, 1)
    mid_bound = placed([mid_bound, swap(mid_bound, near)], place // near, 1)
    first_input = jnp.concatenate([first_state[:, :k_zero], mid_bound], axis=1)

    box_bound = rounded(contract(first_input, down_one))
    box_input = jnp.concatenate([box_state[:, :inner_dev], box_bound], axis=1)
    leaf_bound = rounded(contract(box_input, box_down)).reshape(rhs_count, leaves, edge_count)
    lifted = jnp.einsum(
        "rle,leq->rlq",
        leaf_bound,
        leaf_lift.reshape(leaves, edge_count, points),
        preferred_element_type=jnp.float32,
    )
    particular = jnp.einsum(
        "rlq,lqp->rlp",
        source,
        leaf_particular.reshape(leaves, points, points),
        preferred_element_type=jnp.float32,
    )
    return lifted + particular


def solution(mesh):
    return jax.shard_map(
        per_device,
        mesh=mesh,
        in_specs=(P(None, AXES, None),) + (P(AXES, None),) * 11,
        out_specs=P(None, AXES, None),
        check_vma=False,
    )
```

```python
import jax
import jax.numpy as jnp
from jax import lax
from jax.experimental import pallas as pl
from jax.experimental.pallas import tpu as pltpu
from jax.sharding import PartitionSpec as P

AXES = ("gx", "gy")


def contract(left, right):
    return lax.dot_general(
        left, right, (((1,), (1,)), ((), ())), preferred_element_type=jnp.float32
    )


def product(left, right):
    return jnp.dot(left, right, preferred_element_type=jnp.float32)


def rounded(value):
    return value.astype(jnp.bfloat16)


def swap(value, mask):
    count = lax.axis_size(AXES)
    return lax.ppermute(value, AXES, [(i, i ^ mask) for i in range(count)])


def partner_sum(total, mask):
    return total + swap(rounded(total), mask).astype(jnp.float32)


def bits_of(first, last):
    bits = []
    while first < last:
        bits.append(first)
        first *= 2
    return bits


def placed(pieces, place, axis):
    bit = len(pieces) // 2
    if bit == 0:
        return pieces[0]
    low, high = placed(pieces[:bit], place, axis), placed(pieces[bit:], place, axis)
    upper = place & bit != 0
    return jnp.concatenate(
        [jnp.where(upper, high, low), jnp.where(upper, low, high)], axis=axis
    )


def joined_pair(joined, other, upper, axis):
    return jnp.stack(
        [jnp.where(upper, other, joined), jnp.where(upper, joined, other)], axis=axis
    )


def tie(*values):
    return lax.optimization_barrier(values)


def fetch(sources, scratch, sems):
    copies = [
        pltpu.make_async_copy(source, space, sems.at[i])
        for i, (source, space) in enumerate(zip(sources, scratch))
    ]
    for copy in copies:
        copy.start()
    return copies


def head_kernel(source_hbm, flux_hbm, up_hbm, one_hbm, state_ref, term_ref, low_ref, *rest):
    *scratch, sems = rest
    source, leaf_flux, box_up, up_one = scratch
    copies = fetch((source_hbm, flux_hbm, up_hbm, one_hbm), scratch, sems)
    rhs_count, leaves, points = source.shape
    edge_count = leaf_flux.shape[0] // leaves
    copies[0].wait()
    copies[1].wait()
    rows = source[...].reshape(rhs_count * leaves, points)
    every = contract(rows, leaf_flux[...]).reshape(rhs_count, leaves, leaves * edge_count)
    leaf = lax.broadcasted_iota(jnp.int32, every.shape, 1)
    column = lax.broadcasted_iota(jnp.int32, every.shape, 2)
    own = (column >= leaf * edge_count) & (column < leaf * edge_count + edge_count)
    flux = rounded(jnp.sum(jnp.where(own, every, 0.0), axis=1))
    copies[2].wait()
    state = rounded(contract(flux, box_up[...]))
    state_ref[...] = state
    copies[3].wait()
    term = product(state[:, state.shape[1] - up_one.shape[0] :], up_one[...])
    term_ref[...] = term
    low_ref[...] = rounded(term)


def head(source, leaf_flux, box_up, up_one):
    operands = (source, leaf_flux, box_up, up_one)
    rhs_count = source.shape[0]
    term = (rhs_count, up_one.shape[1])
    return pl.pallas_call(
        head_kernel,
        out_shape=(
            jax.ShapeDtypeStruct((rhs_count, box_up.shape[0]), jnp.bfloat16),
            jax.ShapeDtypeStruct(term, jnp.float32),
            jax.ShapeDtypeStruct(term, jnp.bfloat16),
        ),
        in_specs=[pl.BlockSpec(memory_space=pl.ANY)] * 4,
        scratch_shapes=[pltpu.VMEM(x.shape, x.dtype) for x in operands]
        + [pltpu.SemaphoreType.DMA((4,))],
        compiler_params=pltpu.CompilerParams(vmem_limit_bytes=2**24),
        cost_estimate=pl.CostEstimate(
            flops=2 * rhs_count * sum(x.size for x in operands[1:]),
            bytes_accessed=2 * sum(x.size for x in operands),
            transcendentals=0,
        ),
    )(*operands)


def tail_kernel(
    first_ref, mid_ref, box_ref, particular_ref, one_hbm, down_hbm, lift_hbm, out_ref, *rest
):
    *scratch, sems = rest
    down_one, box_down, leaf_lift = scratch
    copies = fetch((one_hbm, down_hbm, lift_hbm), scratch, sems)
    leaves = out_ref.shape[1]
    edge_count = leaf_lift.shape[0] // leaves
    inner, inner_dev = first_ref.shape[1], box_ref.shape[1]
    copies[0].wait()
    bound = rounded(
        contract(first_ref[...], down_one[:, :inner]) + contract(mid_ref[...], down_one[:, inner:])
    )
    copies[1].wait()
    edges = rounded(
        contract(box_ref[...], box_down[:, :inner_dev]) + contract(bound, box_down[:, inner_dev:])
    )
    copies[2].wait()
    pair_count = 2 * edge_count
    column = lax.broadcasted_iota(jnp.int32, (edges.shape[0], pair_count), 1)
    for leaf in range(leaves):
        start = leaf // 2 * pair_count
        both = edges[:, start : start + pair_count].astype(jnp.float32)
        mine = (column < edge_count) if leaf % 2 == 0 else (column >= edge_count)
        part = rounded(jnp.where(mine, both, 0.0))
        lifted = product(part, leaf_lift[start : start + pair_count, :])
        out_ref[:, leaf, :] = lifted + particular_ref[leaf]


def tail(first_inner, mid_bound, box_inner, particular, down_one, box_down, leaf_lift):
    leaves, rhs_count, points = particular.shape
    weights = (down_one, box_down, leaf_lift)
    return pl.pallas_call(
        tail_kernel,
        out_shape=jax.ShapeDtypeStruct((rhs_count, leaves, points), jnp.float32),
        in_specs=[pl.BlockSpec(memory_space=pltpu.VMEM)] * 4
        + [pl.BlockSpec(memory_space=pl.ANY)] * 3,
        out_specs=pl.BlockSpec(memory_space=pltpu.VMEM),
        scratch_shapes=[pltpu.VMEM(x.shape, x.dtype) for x in weights]
        + [pltpu.SemaphoreType.DMA((3,))],
        compiler_params=pltpu.CompilerParams(vmem_limit_bytes=2**24),
        cost_estimate=pl.CostEstimate(
            flops=2 * rhs_count * sum(x.size for x in weights),
            bytes_accessed=2 * sum(x.size for x in weights) + 8 * particular.size,
            transcendentals=0,
        ),
    )(first_inner, mid_bound, box_inner, particular, *weights)


def per_device(
    source,
    leaf_flux,
    leaf_particular,
    leaf_lift,
    box_up,
    box_down,
    up_one,
    down_one,
    up_two,
    down_two,
    up_root,
    down_root,
):
    rhs_count, leaves, points = source.shape
    count = lax.axis_size(AXES)
    place = lax.axis_index(AXES)
    k_zero = up_one.shape[0]
    inner_dev = box_up.shape[0] - k_zero
    k_one = up_one.shape[1] - k_zero
    width = up_two.shape[0]
    quad = k_one // width
    family = (up_two.shape[1] - k_one) // up_root.shape[0]
    near = quad // 2
    pair = family // 2
    root_points = up_root.shape[1]

    far = pair // 2

    box_state, first_sum, first_low = head(source, leaf_flux, box_up, up_one)

    roots = jnp.concatenate([up_root, down_root], axis=1)
    roots_far = swap(roots, far)
    first_sum = first_sum + swap(first_low, 1).astype(jnp.float32)

    first_sum, roots_far = tie(first_sum, roots_far)
    roots = joined_pair(roots, roots_far, place & far != 0, 0)
    roots_one = swap(roots, 1)
    first_sum = partner_sum(first_sum, near)
    first_state = rounded(first_sum)

    piece = lax.dynamic_slice_in_dim(first_state, k_zero + place % quad * width, width, 1)
    second_sum = product(piece, up_two)
    second_sum, roots_one = tie(second_sum, roots_one)
    roots = joined_pair(roots, roots_one, place & 1 != 0, 1)
    roots_near = swap(roots, near)
    second_sum = partner_sum(second_sum, far | pair)

    second_sum = partner_sum(second_sum, 1 | pair)
    second_sum, roots_near = tie(second_sum, roots_near)
    roots = joined_pair(roots, roots_near, place & near != 0, 1)
    roots_pair = swap(roots, pair)
    second_sum = partner_sum(second_sum, near | pair)
    second_sum = partner_sum(second_sum, pair)
    second_state = rounded(second_sum)
    roots = joined_pair(roots, roots_pair, place & pair != 0, 0)
    roots = roots.reshape(-1, roots.shape[-1])

    root_sum = product(second_state[:, k_one:], roots[:, :root_points])
    for bit in bits_of(family, count):
        root_sum = partner_sum(root_sum, bit | pair)
    root_state = rounded(root_sum)

    top_bound = rounded(contract(root_state, roots[:, root_points:]))
    second_input = jnp.concatenate([second_state[:, :k_one], top_bound], axis=1)
    mid_bound = rounded(contract(second_input, down_two))
    mid_bound = placed([mid_bound, swap(mid_bound, 1)], place, 1)
    mid_bound = placed([mid_bound, swap(mid_bound, near)], place // near, 1)
    particular = jnp.einsum(
        "rlq,lqp->lrp",
        source,
        leaf_particular.reshape(leaves, points, points),
        preferred_element_type=jnp.float32,
    )
    return tail(
        first_state[:, :k_zero],
        mid_bound,
        box_state[:, :inner_dev],
        particular,
        down_one,
        box_down,
        leaf_lift,
    )


def solution(mesh):
    return jax.shard_map(
        per_device,
        mesh=mesh,
        in_specs=(P(None, AXES, None),) + (P(AXES, None),) * 11,
        out_specs=P(None, AXES, None),
        check_vma=False,
    )
```

```python
import jax
import jax.numpy as jnp
from jax import lax
from jax.experimental import pallas as pl
from jax.experimental.pallas import tpu as pltpu
from jax.sharding import PartitionSpec as P

AXES = ("gx", "gy")


def contract(left, right):
    return lax.dot_general(
        left, right, (((1,), (1,)), ((), ())), preferred_element_type=jnp.float32
    )


def product(left, right):
    return jnp.dot(left, right, preferred_element_type=jnp.float32)


def rounded(value):
    return value.astype(jnp.bfloat16)


def swap(value, mask):
    count = lax.axis_size(AXES)
    return lax.ppermute(value, AXES, [(i, i ^ mask) for i in range(count)])


def partner_sum(total, mask):
    return total + swap(rounded(total), mask).astype(jnp.float32)


def bits_of(first, last):
    bits = []
    while first < last:
        bits.append(first)
        first *= 2
    return bits


def placed(pieces, place, axis):
    bit = len(pieces) // 2
    if bit == 0:
        return pieces[0]
    low, high = placed(pieces[:bit], place, axis), placed(pieces[bit:], place, axis)
    upper = place & bit != 0
    return jnp.concatenate(
        [jnp.where(upper, high, low), jnp.where(upper, low, high)], axis=axis
    )


def joined_pair(joined, other, upper, axis):
    return jnp.stack(
        [jnp.where(upper, other, joined), jnp.where(upper, joined, other)], axis=axis
    )


def tie(*values):
    return lax.optimization_barrier(values)


def fetch(sources, scratch, sems):
    copies = [
        pltpu.make_async_copy(source, space, sems.at[i])
        for i, (source, space) in enumerate(zip(sources, scratch))
    ]
    for copy in copies:
        copy.start()
    return copies


def head_kernel(source_hbm, flux_hbm, up_hbm, one_hbm, state_ref, term_ref, low_ref, *rest):
    *scratch, sems = rest
    source, leaf_flux, box_up, up_one = scratch
    copies = fetch((source_hbm, flux_hbm, up_hbm, one_hbm), scratch, sems)
    rhs_count, leaves, points = source.shape
    edge_count = leaf_flux.shape[0] // leaves
    copies[0].wait()
    copies[1].wait()
    rows = source[...].reshape(rhs_count * leaves, points)
    every = contract(rows, leaf_flux[...]).reshape(rhs_count, leaves, leaves * edge_count)
    leaf = lax.broadcasted_iota(jnp.int32, every.shape, 1)
    column = lax.broadcasted_iota(jnp.int32, every.shape, 2)
    own = (column >= leaf * edge_count) & (column < leaf * edge_count + edge_count)
    flux = rounded(jnp.sum(jnp.where(own, every, 0.0), axis=1))
    copies[2].wait()
    state = rounded(contract(flux, box_up[...]))
    state_ref[...] = state
    copies[3].wait()
    term = product(state[:, state.shape[1] - up_one.shape[0] :], up_one[...])
    term_ref[...] = term
    low_ref[...] = rounded(term)


def head(source, leaf_flux, box_up, up_one):
    operands = (source, leaf_flux, box_up, up_one)
    rhs_count = source.shape[0]
    term = (rhs_count, up_one.shape[1])
    return pl.pallas_call(
        head_kernel,
        out_shape=(
            jax.ShapeDtypeStruct((rhs_count, box_up.shape[0]), jnp.bfloat16),
            jax.ShapeDtypeStruct(term, jnp.float32),
            jax.ShapeDtypeStruct(term, jnp.bfloat16),
        ),
        in_specs=[pl.BlockSpec(memory_space=pl.ANY)] * 4,
        scratch_shapes=[pltpu.VMEM(x.shape, x.dtype) for x in operands]
        + [pltpu.SemaphoreType.DMA((4,))],
        cost_estimate=pl.CostEstimate(
            flops=2 * rhs_count * sum(x.size for x in operands[1:]),
            bytes_accessed=2 * sum(x.size for x in operands),
            transcendentals=0,
        ),
    )(*operands)


def tail_kernel(
    first_ref, mid_ref, box_ref, one_hbm, down_hbm, lift_hbm, particular_hbm, out_ref, *rest
):
    *scratch, sems = rest
    down_one, box_down, leaf_lift, particular = scratch
    copies = fetch((one_hbm, down_hbm, lift_hbm, particular_hbm), scratch, sems)
    leaves = out_ref.shape[1]
    edge_count = leaf_lift.shape[0] // leaves
    inner, inner_dev = first_ref.shape[1], box_ref.shape[1]
    copies[0].wait()
    bound = rounded(
        contract(first_ref[...], down_one[:, :inner]) + contract(mid_ref[...], down_one[:, inner:])
    )
    copies[1].wait()
    edges = rounded(
        contract(box_ref[...], box_down[:, :inner_dev]) + contract(bound, box_down[:, inner_dev:])
    )
    copies[2].wait()
    copies[3].wait()
    pair_count = 2 * edge_count
    column = lax.broadcasted_iota(jnp.int32, (edges.shape[0], pair_count), 1)
    for leaf in range(leaves):
        start = leaf // 2 * pair_count
        both = edges[:, start : start + pair_count].astype(jnp.float32)
        mine = (column < edge_count) if leaf % 2 == 0 else (column >= edge_count)
        part = rounded(jnp.where(mine, both, 0.0))
        lifted = product(part, leaf_lift[start : start + pair_count, :])
        out_ref[:, leaf, :] = lifted + particular[leaf]


def tail(first_inner, mid_bound, box_inner, particular, down_one, box_down, leaf_lift):
    leaves, rhs_count, points = particular.shape
    weights = (down_one, box_down, leaf_lift)
    fetched = weights + (particular,)
    return pl.pallas_call(
        tail_kernel,
        out_shape=jax.ShapeDtypeStruct((rhs_count, leaves, points), jnp.float32),
        in_specs=[pl.BlockSpec(memory_space=pltpu.VMEM)] * 3
        + [pl.BlockSpec(memory_space=pl.ANY)] * 4,
        out_specs=pl.BlockSpec(memory_space=pltpu.VMEM),
        scratch_shapes=[pltpu.VMEM(x.shape, x.dtype) for x in fetched]
        + [pltpu.SemaphoreType.DMA((4,))],
        cost_estimate=pl.CostEstimate(
            flops=2 * rhs_count * sum(x.size for x in weights),
            bytes_accessed=2 * sum(x.size for x in weights) + 8 * particular.size,
            transcendentals=0,
        ),
    )(first_inner, mid_bound, box_inner, *fetched)


def per_device(
    source,
    leaf_flux,
    leaf_particular,
    leaf_lift,
    box_up,
    box_down,
    up_one,
    down_one,
    up_two,
    down_two,
    up_root,
    down_root,
):
    rhs_count, leaves, points = source.shape
    count = lax.axis_size(AXES)
    place = lax.axis_index(AXES)
    k_zero = up_one.shape[0]
    inner_dev = box_up.shape[0] - k_zero
    k_one = up_one.shape[1] - k_zero
    width = up_two.shape[0]
    quad = k_one // width
    family = (up_two.shape[1] - k_one) // up_root.shape[0]
    near = quad // 2
    pair = family // 2
    root_points = up_root.shape[1]

    far = pair // 2

    box_state, first_sum, first_low = head(source, leaf_flux, box_up, up_one)

    roots = jnp.concatenate([up_root, down_root], axis=1)
    roots_far = swap(roots, far)
    first_sum = first_sum + swap(first_low, 1).astype(jnp.float32)

    first_sum, roots_far = tie(first_sum, roots_far)
    roots = joined_pair(roots, roots_far, place & far != 0, 0)
    roots_one = swap(roots, 1)
    first_sum = partner_sum(first_sum, near)
    first_state = rounded(first_sum)

    piece = lax.dynamic_slice_in_dim(first_state, k_zero + place % quad * width, width, 1)
    second_sum = product(piece, up_two)
    second_sum, roots_one = tie(second_sum, roots_one)
    roots = joined_pair(roots, roots_one, place & 1 != 0, 1)
    roots_near = swap(roots, near)
    second_sum = partner_sum(second_sum, far | pair)

    second_sum = partner_sum(second_sum, 1 | pair)
    second_sum, roots_near = tie(second_sum, roots_near)
    roots = joined_pair(roots, roots_near, place & near != 0, 1)
    roots_pair = swap(roots, pair)
    second_sum = partner_sum(second_sum, near | pair)
    second_sum = partner_sum(second_sum, pair)
    second_state = rounded(second_sum)
    roots = joined_pair(roots, roots_pair, place & pair != 0, 0)
    roots = roots.reshape(-1, roots.shape[-1])

    root_sum = product(second_state[:, k_one:], roots[:, :root_points])
    for bit in bits_of(family, count):
        root_sum = partner_sum(root_sum, bit | pair)
    root_state = rounded(root_sum)

    top_bound = rounded(contract(root_state, roots[:, root_points:]))
    second_input = jnp.concatenate([second_state[:, :k_one], top_bound], axis=1)
    mid_bound = rounded(contract(second_input, down_two))
    mid_bound = placed([mid_bound, swap(mid_bound, 1)], place, 1)
    mid_bound = placed([mid_bound, swap(mid_bound, near)], place // near, 1)
    particular = jnp.einsum(
        "rlq,lqp->lrp",
        source,
        leaf_particular.reshape(leaves, points, points),
        preferred_element_type=jnp.float32,
    )
    return tail(
        first_state[:, :k_zero],
        mid_bound,
        box_state[:, :inner_dev],
        particular,
        down_one,
        box_down,
        leaf_lift,
    )


def solution(mesh):
    return jax.shard_map(
        per_device,
        mesh=mesh,
        in_specs=(P(None, AXES, None),) + (P(AXES, None),) * 11,
        out_specs=P(None, AXES, None),
        check_vma=False,
    )
```

```python
import jax
import jax.numpy as jnp
from jax import lax
from jax.experimental import pallas as pl
from jax.experimental.pallas import tpu as pltpu
from jax.sharding import PartitionSpec as P

AXES = ("gx", "gy")


def contract(left, right):
    return lax.dot_general(
        left, right, (((1,), (1,)), ((), ())), preferred_element_type=jnp.float32
    )


def product(left, right):
    return jnp.dot(left, right, preferred_element_type=jnp.float32)


def rounded(value):
    return value.astype(jnp.bfloat16)


def swap(value, mask):
    count = lax.axis_size(AXES)
    return lax.ppermute(value, AXES, [(i, i ^ mask) for i in range(count)])


def partner_sum(total, mask):
    return total + swap(rounded(total), mask).astype(jnp.float32)


def bits_of(first, last):
    bits = []
    while first < last:
        bits.append(first)
        first *= 2
    return bits


def placed(pieces, place, axis):
    bit = len(pieces) // 2
    if bit == 0:
        return pieces[0]
    low, high = placed(pieces[:bit], place, axis), placed(pieces[bit:], place, axis)
    upper = place & bit != 0
    return jnp.concatenate(
        [jnp.where(upper, high, low), jnp.where(upper, low, high)], axis=axis
    )


def joined_pair(joined, other, upper, axis):
    return jnp.stack(
        [jnp.where(upper, other, joined), jnp.where(upper, joined, other)], axis=axis
    )


def fetch(sources, scratch, sems):
    copies = [
        pltpu.make_async_copy(source, space, sems.at[i])
        for i, (source, space) in enumerate(zip(sources, scratch))
    ]
    for copy in copies:
        copy.start()
    return copies


def head_kernel(source_hbm, flux_hbm, up_hbm, one_hbm, state_ref, term_ref, low_ref, *rest):
    *scratch, sems = rest
    source, leaf_flux, box_up, up_one = scratch
    copies = fetch((source_hbm, flux_hbm, up_hbm, one_hbm), scratch, sems)
    rhs_count, leaves, points = source.shape
    edge_count = leaf_flux.shape[0] // leaves
    copies[0].wait()
    copies[1].wait()
    rows = source[...].reshape(rhs_count * leaves, points)
    every = contract(rows, leaf_flux[...]).reshape(rhs_count, leaves, leaves * edge_count)
    leaf = lax.broadcasted_iota(jnp.int32, every.shape, 1)
    column = lax.broadcasted_iota(jnp.int32, every.shape, 2)
    own = (column >= leaf * edge_count) & (column < leaf * edge_count + edge_count)
    flux = rounded(jnp.sum(jnp.where(own, every, 0.0), axis=1))
    copies[2].wait()
    state = rounded(contract(flux, box_up[...]))
    state_ref[...] = state
    copies[3].wait()
    term = product(state[:, state.shape[1] - up_one.shape[0] :], up_one[...])
    term_ref[...] = term
    low_ref[...] = rounded(term)


def head(source, leaf_flux, box_up, up_one):
    operands = (source, leaf_flux, box_up, up_one)
    rhs_count = source.shape[0]
    term = (rhs_count, up_one.shape[1])
    return pl.pallas_call(
        head_kernel,
        out_shape=(
            jax.ShapeDtypeStruct((rhs_count, box_up.shape[0]), jnp.bfloat16),
            jax.ShapeDtypeStruct(term, jnp.float32),
            jax.ShapeDtypeStruct(term, jnp.bfloat16),
        ),
        in_specs=[pl.BlockSpec(memory_space=pl.ANY)] * 4,
        scratch_shapes=[pltpu.VMEM(x.shape, x.dtype) for x in operands]
        + [pltpu.SemaphoreType.DMA((4,))],
        cost_estimate=pl.CostEstimate(
            flops=2 * rhs_count * sum(x.size for x in operands[1:]),
            bytes_accessed=2 * sum(x.size for x in operands),
            transcendentals=0,
        ),
    )(*operands)


def tail_kernel(
    first_ref, mid_ref, box_ref, one_hbm, down_hbm, lift_hbm, particular_hbm, out_ref, *rest
):
    *scratch, sems = rest
    down_one, box_down, leaf_lift, particular = scratch
    copies = fetch((one_hbm, down_hbm, lift_hbm, particular_hbm), scratch, sems)
    leaves = out_ref.shape[1]
    edge_count = leaf_lift.shape[0] // leaves
    inner, inner_dev = first_ref.shape[1], box_ref.shape[1]
    copies[0].wait()
    bound = rounded(
        contract(first_ref[...], down_one[:, :inner]) + contract(mid_ref[...], down_one[:, inner:])
    )
    copies[1].wait()
    edges = rounded(
        contract(box_ref[...], box_down[:, :inner_dev]) + contract(bound, box_down[:, inner_dev:])
    )
    copies[2].wait()
    copies[3].wait()
    pair_count = 2 * edge_count
    column = lax.broadcasted_iota(jnp.int32, (edges.shape[0], pair_count), 1)
    for leaf in range(leaves):
        start = leaf // 2 * pair_count
        both = edges[:, start : start + pair_count].astype(jnp.float32)
        mine = (column < edge_count) if leaf % 2 == 0 else (column >= edge_count)
        part = rounded(jnp.where(mine, both, 0.0))
        lifted = product(part, leaf_lift[start : start + pair_count, :])
        out_ref[:, leaf, :] = lifted + particular[leaf]


def tail(first_inner, mid_bound, box_inner, particular, down_one, box_down, leaf_lift):
    leaves, rhs_count, points = particular.shape
    weights = (down_one, box_down, leaf_lift)
    fetched = weights + (particular,)
    return pl.pallas_call(
        tail_kernel,
        out_shape=jax.ShapeDtypeStruct((rhs_count, leaves, points), jnp.float32),
        in_specs=[pl.BlockSpec(memory_space=pltpu.VMEM)] * 3
        + [pl.BlockSpec(memory_space=pl.ANY)] * 4,
        out_specs=pl.BlockSpec(memory_space=pltpu.VMEM),
        scratch_shapes=[pltpu.VMEM(x.shape, x.dtype) for x in fetched]
        + [pltpu.SemaphoreType.DMA((4,))],
        cost_estimate=pl.CostEstimate(
            flops=2 * rhs_count * sum(x.size for x in weights),
            bytes_accessed=2 * sum(x.size for x in weights) + 8 * particular.size,
            transcendentals=0,
        ),
    )(first_inner, mid_bound, box_inner, *fetched)


def per_device(
    source,
    leaf_flux,
    leaf_particular,
    leaf_lift,
    box_up,
    box_down,
    up_one,
    down_one,
    up_two,
    down_two,
    up_root,
    down_root,
):
    rhs_count, leaves, points = source.shape
    count = lax.axis_size(AXES)
    place = lax.axis_index(AXES)
    k_zero = up_one.shape[0]
    inner_dev = box_up.shape[0] - k_zero
    k_one = up_one.shape[1] - k_zero
    width = up_two.shape[0]
    quad = k_one // width
    family = (up_two.shape[1] - k_one) // up_root.shape[0]
    near = quad // 2
    pair = family // 2
    root_points = up_root.shape[1]

    far = pair // 2

    box_state, first_sum, first_low = head(source, leaf_flux, box_up, up_one)

    roots = jnp.concatenate([up_root, down_root], axis=1)
    roots_far = swap(roots, far)
    first_sum = first_sum + swap(first_low, 1).astype(jnp.float32)

    roots = joined_pair(roots, roots_far, place & far != 0, 0)
    roots_one = swap(roots, 1)
    first_sum = partner_sum(first_sum, near)
    first_state = rounded(first_sum)

    piece = lax.dynamic_slice_in_dim(first_state, k_zero + place % quad * width, width, 1)
    second_sum = product(piece, up_two)
    roots = joined_pair(roots, roots_one, place & 1 != 0, 1)
    roots_near = swap(roots, near)
    second_sum = partner_sum(second_sum, far | pair)

    second_sum = partner_sum(second_sum, 1 | pair)
    roots = joined_pair(roots, roots_near, place & near != 0, 1)
    roots_pair = swap(roots, pair)
    second_sum = partner_sum(second_sum, near | pair)
    second_sum = partner_sum(second_sum, pair)
    second_state = rounded(second_sum)
    roots = joined_pair(roots, roots_pair, place & pair != 0, 0)
    roots = roots.reshape(-1, roots.shape[-1])

    root_sum = product(second_state[:, k_one:], roots[:, :root_points])
    for bit in bits_of(family, count):
        root_sum = partner_sum(root_sum, bit | pair)
    root_state = rounded(root_sum)

    top_bound = rounded(contract(root_state, roots[:, root_points:]))
    second_input = jnp.concatenate([second_state[:, :k_one], top_bound], axis=1)
    mid_bound = rounded(contract(second_input, down_two))
    mid_bound = placed([mid_bound, swap(mid_bound, 1)], place, 1)
    mid_bound = placed([mid_bound, swap(mid_bound, near)], place // near, 1)
    particular = jnp.einsum(
        "rlq,lqp->lrp",
        source,
        leaf_particular.reshape(leaves, points, points),
        preferred_element_type=jnp.float32,
    )
    return tail(
        first_state[:, :k_zero],
        mid_bound,
        box_state[:, :inner_dev],
        particular,
        down_one,
        box_down,
        leaf_lift,
    )


def solution(mesh):
    return jax.shard_map(
        per_device,
        mesh=mesh,
        in_specs=(P(None, AXES, None),) + (P(AXES, None),) * 11,
        out_specs=P(None, AXES, None),
        check_vma=False,
    )
```

```python
import jax
import jax.numpy as jnp
from jax import lax
from jax.sharding import PartitionSpec as P

AXES = ("gx", "gy")


def contract(left, right):
    return lax.dot_general(
        left, right, (((1,), (1,)), ((), ())), preferred_element_type=jnp.float32
    )


def product(left, right):
    return jnp.dot(left, right, preferred_element_type=jnp.float32)


def rounded(value):
    return value.astype(jnp.bfloat16)


def swap(value, mask):
    count = lax.axis_size(AXES)
    return lax.ppermute(value, AXES, [(i, i ^ mask) for i in range(count)])


def partner_sum(total, mask):
    return total + swap(rounded(total), mask).astype(jnp.float32)


def bits_of(first, last):
    bits = []
    while first < last:
        bits.append(first)
        first *= 2
    return bits


def placed(pieces, place, axis):
    bit = len(pieces) // 2
    if bit == 0:
        return pieces[0]
    low, high = placed(pieces[:bit], place, axis), placed(pieces[bit:], place, axis)
    upper = place & bit != 0
    return jnp.concatenate(
        [jnp.where(upper, high, low), jnp.where(upper, low, high)], axis=axis
    )


def joined_pair(joined, other, upper, axis):
    return jnp.stack(
        [jnp.where(upper, other, joined), jnp.where(upper, joined, other)], axis=axis
    )


def per_device(
    source,
    leaf_flux,
    leaf_particular,
    leaf_lift,
    box_up,
    box_down,
    up_one,
    down_one,
    up_two,
    down_two,
    up_root,
    down_root,
):
    rhs_count, leaves, points = source.shape
    edge_count = leaf_flux.shape[0] // leaves
    count = lax.axis_size(AXES)
    place = lax.axis_index(AXES)
    k_zero = up_one.shape[0]
    inner_dev = box_up.shape[0] - k_zero
    k_one = up_one.shape[1] - k_zero
    width = up_two.shape[0]
    quad = k_one // width
    family = (up_two.shape[1] - k_one) // up_root.shape[0]
    near = quad // 2
    pair = family // 2
    root_points = up_root.shape[1]

    far = pair // 2

    flux = jnp.einsum(
        "rlq,leq->rle",
        source,
        leaf_flux.reshape(leaves, edge_count, points),
        preferred_element_type=jnp.float32,
    )
    flux = rounded(flux).reshape(rhs_count, leaves * edge_count)
    box_state = rounded(contract(flux, box_up))
    first_sum = product(box_state[:, inner_dev:], up_one)

    roots = jnp.concatenate([up_root, down_root], axis=1)
    roots_far = swap(roots, far)
    first_sum = partner_sum(first_sum, 1)

    roots = joined_pair(roots, roots_far, place & far != 0, 0)
    roots_one = swap(roots, 1)
    first_sum = partner_sum(first_sum, near)
    first_state = rounded(first_sum)

    piece = lax.dynamic_slice_in_dim(first_state, k_zero + place % quad * width, width, 1)
    second_sum = product(piece, up_two)
    roots = joined_pair(roots, roots_one, place & 1 != 0, 1)
    roots_near = swap(roots, near)
    second_sum = partner_sum(second_sum, far | pair)

    second_sum = partner_sum(second_sum, 1 | pair)
    roots = joined_pair(roots, roots_near, place & near != 0, 1)
    roots_pair = swap(roots, pair)
    second_sum = partner_sum(second_sum, near | pair)
    second_sum = partner_sum(second_sum, pair)
    second_state = rounded(second_sum)
    roots = joined_pair(roots, roots_pair, place & pair != 0, 0)
    roots = roots.reshape(-1, roots.shape[-1])

    root_sum = product(second_state[:, k_one:], roots[:, :root_points])
    for bit in bits_of(family, count):
        root_sum = partner_sum(root_sum, bit | pair)
    root_state = rounded(root_sum)

    top_bound = rounded(contract(root_state, roots[:, root_points:]))
    second_input = jnp.concatenate([second_state[:, :k_one], top_bound], axis=1)
    mid_bound = rounded(contract(second_input, down_two))
    mid_bound = placed([mid_bound, swap(mid_bound, 1)], place, 1)
    mid_bound = placed([mid_bound, swap(mid_bound, near)], place // near, 1)
    first_input = jnp.concatenate([first_state[:, :k_zero], mid_bound], axis=1)

    box_bound = rounded(contract(first_input, down_one))
    box_input = jnp.concatenate([box_state[:, :inner_dev], box_bound], axis=1)
    leaf_bound = rounded(contract(box_input, box_down)).reshape(rhs_count, leaves, edge_count)
    lifted = jnp.einsum(
        "rle,leq->rlq",
        leaf_bound,
        leaf_lift.reshape(leaves, edge_count, points),
        preferred_element_type=jnp.float32,
    )
    particular = jnp.einsum(
        "rlq,lqp->rlp",
        source,
        leaf_particular.reshape(leaves, points, points),
        preferred_element_type=jnp.float32,
    )
    return lifted + particular


def solution(mesh):
    return jax.shard_map(
        per_device,
        mesh=mesh,
        in_specs=(P(None, AXES, None),) + (P(AXES, None),) * 11,
        out_specs=P(None, AXES, None),
        check_vma=False,
    )
```

```python
import jax
import jax.numpy as jnp
from jax import lax
from jax.sharding import PartitionSpec as P

AXES = ("gx", "gy")


def contract(left, right):
    return lax.dot_general(
        left, right, (((1,), (1,)), ((), ())), preferred_element_type=jnp.float32
    )


def product(left, right):
    return jnp.dot(left, right, preferred_element_type=jnp.float32)


def rounded(value):
    return value.astype(jnp.bfloat16)


def swap(value, mask):
    count = lax.axis_size(AXES)
    return lax.ppermute(value, AXES, [(i, i ^ mask) for i in range(count)])


def partner_sum(total, mask):
    return total + swap(rounded(total), mask).astype(jnp.float32)


def bits_of(first, last):
    bits = []
    while first < last:
        bits.append(first)
        first *= 2
    return bits


def placed(pieces, place, axis):
    bit = len(pieces) // 2
    if bit == 0:
        return pieces[0]
    low, high = placed(pieces[:bit], place, axis), placed(pieces[bit:], place, axis)
    upper = place & bit != 0
    return jnp.concatenate(
        [jnp.where(upper, high, low), jnp.where(upper, low, high)], axis=axis
    )


def joined_pair(joined, other, upper, axis):
    return jnp.stack(
        [jnp.where(upper, other, joined), jnp.where(upper, joined, other)], axis=axis
    )


def per_device(
    source,
    leaf_flux,
    leaf_particular,
    leaf_lift,
    box_up,
    box_down,
    up_one,
    down_one,
    up_two,
    down_two,
    up_root,
    down_root,
):
    rhs_count, leaves, points = source.shape
    edge_count = leaf_flux.shape[0] // leaves
    count = lax.axis_size(AXES)
    place = lax.axis_index(AXES)
    k_zero = up_one.shape[0]
    inner_dev = box_up.shape[0] - k_zero
    k_one = up_one.shape[1] - k_zero
    width = up_two.shape[0]
    quad = k_one // width
    family = (up_two.shape[1] - k_one) // up_root.shape[0]
    near = quad // 2
    pair = family // 2
    root_points = up_root.shape[1]

    far = pair // 2

    flux = jnp.einsum(
        "rlq,leq->rle",
        source,
        leaf_flux.reshape(leaves, edge_count, points),
        preferred_element_type=jnp.float32,
    )
    flux = rounded(flux).reshape(rhs_count, leaves * edge_count)
    box_state = rounded(contract(flux, box_up))
    first_sum = product(box_state[:, inner_dev:], up_one)

    roots = jnp.concatenate([up_root, down_root], axis=1)
    roots_far = swap(roots, far)
    first_sum = partner_sum(first_sum, 1)

    roots = joined_pair(roots, roots_far, place & far != 0, 0)
    roots_one = swap(roots, 1)
    first_sum = partner_sum(first_sum, near)
    first_state = rounded(first_sum)

    piece = lax.dynamic_slice_in_dim(first_state, k_zero + place % quad * width, width, 1)
    second_sum = product(piece, up_two)
    roots = joined_pair(roots, roots_one, place & 1 != 0, 1)
    roots_near, roots_pair = swap(roots, near), swap(roots, pair)
    second_sum = partner_sum(second_sum, far | pair)

    second_sum = partner_sum(second_sum, 1 | pair)
    low = joined_pair(roots, roots_near, place & near != 0, 1)
    high = swap(roots_near, pair)
    second_sum = partner_sum(second_sum, near | pair)
    second_sum, high = lax.optimization_barrier((second_sum, high))
    high = joined_pair(roots_pair, high, place & near != 0, 1)
    second_sum = partner_sum(second_sum, pair)
    second_state = rounded(second_sum)
    roots = joined_pair(low, high, place & pair != 0, 0)
    roots = roots.reshape(-1, roots.shape[-1])

    root_sum = product(second_state[:, k_one:], roots[:, :root_points])
    for bit in bits_of(family, count):
        root_sum = partner_sum(root_sum, bit | pair)
    root_state = rounded(root_sum)

    top_bound = rounded(contract(root_state, roots[:, root_points:]))
    second_input = jnp.concatenate([second_state[:, :k_one], top_bound], axis=1)
    mid_bound = rounded(contract(second_input, down_two))
    mid_bound = placed([mid_bound, swap(mid_bound, 1)], place, 1)
    mid_bound = placed([mid_bound, swap(mid_bound, near)], place // near, 1)
    first_input = jnp.concatenate([first_state[:, :k_zero], mid_bound], axis=1)

    box_bound = rounded(contract(first_input, down_one))
    box_input = jnp.concatenate([box_state[:, :inner_dev], box_bound], axis=1)
    leaf_bound = rounded(contract(box_input, box_down)).reshape(rhs_count, leaves, edge_count)
    lifted = jnp.einsum(
        "rle,leq->rlq",
        leaf_bound,
        leaf_lift.reshape(leaves, edge_count, points),
        preferred_element_type=jnp.float32,
    )
    particular = jnp.einsum(
        "rlq,lqp->rlp",
        source,
        leaf_particular.reshape(leaves, points, points),
        preferred_element_type=jnp.float32,
    )
    return lifted + particular


def solution(mesh):
    return jax.shard_map(
        per_device,
        mesh=mesh,
        in_specs=(P(None, AXES, None),) + (P(AXES, None),) * 11,
        out_specs=P(None, AXES, None),
        check_vma=False,
    )
```

```python
import jax
import jax.numpy as jnp
from jax import lax
from jax.sharding import PartitionSpec as P

AXES = ("gx", "gy")


def contract(left, right):
    return lax.dot_general(
        left, right, (((1,), (1,)), ((), ())), preferred_element_type=jnp.float32
    )


def product(left, right):
    return jnp.dot(left, right, preferred_element_type=jnp.float32)


def rounded(value):
    return value.astype(jnp.bfloat16)


def swap(value, mask):
    count = lax.axis_size(AXES)
    return lax.ppermute(value, AXES, [(i, i ^ mask) for i in range(count)])


def partner_sum(total, mask):
    return total + swap(rounded(total), mask).astype(jnp.float32)


def bits_of(first, last):
    bits = []
    while first < last:
        bits.append(first)
        first *= 2
    return bits


def placed(pieces, place, axis):
    bit = len(pieces) // 2
    if bit == 0:
        return pieces[0]
    low, high = placed(pieces[:bit], place, axis), placed(pieces[bit:], place, axis)
    upper = place & bit != 0
    return jnp.concatenate(
        [jnp.where(upper, high, low), jnp.where(upper, low, high)], axis=axis
    )


def joined_pair(joined, other, upper, axis):
    return jnp.stack(
        [jnp.where(upper, other, joined), jnp.where(upper, joined, other)], axis=axis
    )


def per_device(
    source,
    leaf_flux,
    leaf_particular,
    leaf_lift,
    box_up,
    box_down,
    up_one,
    down_one,
    up_two,
    down_two,
    up_root,
    down_root,
):
    rhs_count, leaves, points = source.shape
    edge_count = leaf_flux.shape[0] // leaves
    count = lax.axis_size(AXES)
    place = lax.axis_index(AXES)
    k_zero = up_one.shape[0]
    inner_dev = box_up.shape[0] - k_zero
    k_one = up_one.shape[1] - k_zero
    width = up_two.shape[0]
    quad = k_one // width
    family = (up_two.shape[1] - k_one) // up_root.shape[0]
    near = quad // 2
    pair = family // 2
    root_points = up_root.shape[1]

    far = pair // 2

    flux = jnp.einsum(
        "rlq,leq->rle",
        source,
        leaf_flux.reshape(leaves, edge_count, points),
        preferred_element_type=jnp.float32,
    )
    flux = rounded(flux).reshape(rhs_count, leaves * edge_count)
    box_state = rounded(contract(flux, box_up))
    first_sum = product(box_state[:, inner_dev:], up_one)

    roots = jnp.concatenate([up_root, down_root], axis=1)
    roots_far = swap(roots, far)
    first_sum = partner_sum(first_sum, 1)

    roots = joined_pair(roots, roots_far, place & far != 0, 0)
    roots = swap(swap(roots, pair), pair)
    roots_one = swap(roots, 1)
    first_sum = partner_sum(first_sum, near)
    first_state = rounded(first_sum)

    piece = lax.dynamic_slice_in_dim(first_state, k_zero + place % quad * width, width, 1)
    second_sum = product(piece, up_two)
    roots = joined_pair(roots, roots_one, place & 1 != 0, 1)
    roots_near, roots_pair = swap(roots, near), swap(roots, pair)
    second_sum = partner_sum(second_sum, far | pair)

    second_sum = partner_sum(second_sum, 1 | pair)
    low = joined_pair(roots, roots_near, place & near != 0, 1)
    high = swap(roots_near, pair)
    second_sum = partner_sum(second_sum, near | pair)
    second_sum, high = lax.optimization_barrier((second_sum, high))
    high = joined_pair(roots_pair, high, place & near != 0, 1)
    second_sum = partner_sum(second_sum, pair)
    second_state = rounded(second_sum)
    roots = joined_pair(low, high, place & pair != 0, 0)
    roots = roots.reshape(-1, roots.shape[-1])

    root_sum = product(second_state[:, k_one:], roots[:, :root_points])
    for bit in bits_of(family, count):
        root_sum = partner_sum(root_sum, bit | pair)
    root_state = rounded(root_sum)

    top_bound = rounded(contract(root_state, roots[:, root_points:]))
    second_input = jnp.concatenate([second_state[:, :k_one], top_bound], axis=1)
    mid_bound = rounded(contract(second_input, down_two))
    mid_bound = placed([mid_bound, swap(mid_bound, 1)], place, 1)
    mid_bound = placed([mid_bound, swap(mid_bound, near)], place // near, 1)
    first_input = jnp.concatenate([first_state[:, :k_zero], mid_bound], axis=1)

    box_bound = rounded(contract(first_input, down_one))
    box_input = jnp.concatenate([box_state[:, :inner_dev], box_bound], axis=1)
    leaf_bound = rounded(contract(box_input, box_down)).reshape(rhs_count, leaves, edge_count)
    lifted = jnp.einsum(
        "rle,leq->rlq",
        leaf_bound,
        leaf_lift.reshape(leaves, edge_count, points),
        preferred_element_type=jnp.float32,
    )
    particular = jnp.einsum(
        "rlq,lqp->rlp",
        source,
        leaf_particular.reshape(leaves, points, points),
        preferred_element_type=jnp.float32,
    )
    return lifted + particular


def solution(mesh):
    return jax.shard_map(
        per_device,
        mesh=mesh,
        in_specs=(P(None, AXES, None),) + (P(AXES, None),) * 11,
        out_specs=P(None, AXES, None),
        check_vma=False,
    )
```

```python
import jax
import jax.numpy as jnp
from jax import lax
from jax.sharding import PartitionSpec as P

AXES = ("gx", "gy")


def contract(left, right):
    return lax.dot_general(
        left, right, (((1,), (1,)), ((), ())), preferred_element_type=jnp.float32
    )


def product(left, right):
    return jnp.dot(left, right, preferred_element_type=jnp.float32)


def rounded(value):
    return value.astype(jnp.bfloat16)


def swap(value, mask):
    count = lax.axis_size(AXES)
    return lax.ppermute(value, AXES, [(i, i ^ mask) for i in range(count)])


def partner_sum(total, mask):
    return total + swap(rounded(total), mask).astype(jnp.float32)


def bits_of(first, last):
    bits = []
    while first < last:
        bits.append(first)
        first *= 2
    return bits


def placed(pieces, place, axis):
    bit = len(pieces) // 2
    if bit == 0:
        return pieces[0]
    low, high = placed(pieces[:bit], place, axis), placed(pieces[bit:], place, axis)
    upper = place & bit != 0
    return jnp.concatenate(
        [jnp.where(upper, high, low), jnp.where(upper, low, high)], axis=axis
    )


def joined_pair(joined, other, upper, axis):
    return jnp.stack(
        [jnp.where(upper, other, joined), jnp.where(upper, joined, other)], axis=axis
    )


def diagonal(rows, leaves):
    columns = rows.shape[2]
    leaf = jnp.arange(columns) // (columns // leaves)
    kept = jnp.where(leaf == jnp.arange(leaves)[:, None], rows, jnp.zeros((), rows.dtype))
    return kept.reshape(-1, columns)


def per_device(
    source,
    leaf_flux,
    leaf_particular,
    leaf_lift,
    box_up,
    box_down,
    up_one,
    down_one,
    up_two,
    down_two,
    up_root,
    down_root,
):
    rhs_count, leaves, points = source.shape
    edge_count = leaf_flux.shape[0] // leaves
    count = lax.axis_size(AXES)
    place = lax.axis_index(AXES)
    k_zero = up_one.shape[0]
    inner_dev = box_up.shape[0] - k_zero
    k_one = up_one.shape[1] - k_zero
    width = up_two.shape[0]
    quad = k_one // width
    family = (up_two.shape[1] - k_one) // up_root.shape[0]
    near = quad // 2
    pair = family // 2
    root_points = up_root.shape[1]

    far = pair // 2

    flux = jnp.einsum(
        "rlq,leq->rle",
        source,
        leaf_flux.reshape(leaves, edge_count, points),
        preferred_element_type=jnp.float32,
    )
    flux = rounded(flux).reshape(rhs_count, leaves * edge_count)
    box_state = rounded(contract(flux, box_up))
    first_sum = product(box_state[:, inner_dev:], up_one)

    roots = jnp.concatenate([up_root, down_root], axis=1)
    roots_far = swap(roots, far)
    first_sum = partner_sum(first_sum, 1)

    roots = joined_pair(roots, roots_far, place & far != 0, 0)
    roots_one = swap(roots, 1)
    first_sum = partner_sum(first_sum, near)
    first_state = rounded(first_sum)

    piece = lax.dynamic_slice_in_dim(first_state, k_zero + place % quad * width, width, 1)
    second_sum = product(piece, up_two)
    roots = joined_pair(roots, roots_one, place & 1 != 0, 1)
    roots_near, roots_pair = swap(roots, near), swap(roots, pair)
    second_sum = partner_sum(second_sum, far | pair)

    second_sum = partner_sum(second_sum, 1 | pair)
    low = joined_pair(roots, roots_near, place & near != 0, 1)
    high = swap(roots_near, pair)
    second_sum = partner_sum(second_sum, near | pair)
    second_sum, high = lax.optimization_barrier((second_sum, high))
    high = joined_pair(roots_pair, high, place & near != 0, 1)
    second_sum = partner_sum(second_sum, pair)
    second_state = rounded(second_sum)
    roots = joined_pair(low, high, place & pair != 0, 0)
    roots = roots.reshape(-1, roots.shape[-1])

    root_sum = product(second_state[:, k_one:], roots[:, :root_points])
    for bit in bits_of(family, count):
        root_sum = partner_sum(root_sum, bit | pair)
    root_state = rounded(root_sum)

    top_bound = rounded(contract(root_state, roots[:, root_points:]))
    second_input = jnp.concatenate([second_state[:, :k_one], top_bound], axis=1)
    mid_bound = rounded(contract(second_input, down_two))
    mid_bound = placed([mid_bound, swap(mid_bound, 1)], place, 1)
    mid_bound = placed([mid_bound, swap(mid_bound, near)], place // near, 1)
    first_input = jnp.concatenate([first_state[:, :k_zero], mid_bound], axis=1)

    box_bound = rounded(contract(first_input, down_one))
    box_input = jnp.concatenate([box_state[:, :inner_dev], box_bound], axis=1)
    leaf_bound = rounded(contract(box_input, box_down))
    edges = diagonal(leaf_bound[:, None, :], leaves)
    lifted = product(edges, leaf_lift)
    particular = jnp.einsum(
        "rlq,lqp->rlp",
        source,
        leaf_particular.reshape(leaves, points, points),
        preferred_element_type=jnp.float32,
    )
    return lifted.reshape(particular.shape) + particular


def solution(mesh):
    return jax.shard_map(
        per_device,
        mesh=mesh,
        in_specs=(P(None, AXES, None),) + (P(AXES, None),) * 11,
        out_specs=P(None, AXES, None),
        check_vma=False,
    )
```

```python
import jax
import jax.numpy as jnp
from jax import lax
from jax.sharding import PartitionSpec as P

AXES = ("gx", "gy")


def contract(left, right):
    return lax.dot_general(
        left, right, (((1,), (1,)), ((), ())), preferred_element_type=jnp.float32
    )


def product(left, right):
    return jnp.dot(left, right, preferred_element_type=jnp.float32)


def rounded(value):
    return value.astype(jnp.bfloat16)


def swap(value, mask):
    count = lax.axis_size(AXES)
    return lax.ppermute(value, AXES, [(i, i ^ mask) for i in range(count)])


def partner_sum(total, mask):
    return total + swap(rounded(total), mask).astype(jnp.float32)


def bits_of(first, last):
    bits = []
    while first < last:
        bits.append(first)
        first *= 2
    return bits


def placed(pieces, place, axis):
    bit = len(pieces) // 2
    if bit == 0:
        return pieces[0]
    low, high = placed(pieces[:bit], place, axis), placed(pieces[bit:], place, axis)
    upper = place & bit != 0
    return jnp.concatenate(
        [jnp.where(upper, high, low), jnp.where(upper, low, high)], axis=axis
    )


def joined_pair(joined, other, upper, axis):
    return jnp.stack(
        [jnp.where(upper, other, joined), jnp.where(upper, joined, other)], axis=axis
    )


def diagonal(rows, leaves):
    columns = rows.shape[2]
    leaf = jnp.arange(columns) // (columns // leaves)
    kept = jnp.where(leaf == jnp.arange(leaves)[:, None], rows, jnp.zeros((), rows.dtype))
    return kept.reshape(-1, columns)


def family_rows(own, own_near, other, other_near, near, pair, place):
    own = joined_pair(own, own_near, place & near != 0, 1)
    other = joined_pair(other, other_near, place & near != 0, 1)
    rows = joined_pair(own, other, place & pair != 0, 0)
    return rows.reshape(-1, rows.shape[-1])


def per_device(
    source,
    leaf_flux,
    leaf_particular,
    leaf_lift,
    box_up,
    box_down,
    up_one,
    down_one,
    up_two,
    down_two,
    up_root,
    down_root,
):
    rhs_count, leaves, points = source.shape
    edge_count = leaf_flux.shape[0] // leaves
    count = lax.axis_size(AXES)
    place = lax.axis_index(AXES)
    k_zero = up_one.shape[0]
    inner_dev = box_up.shape[0] - k_zero
    k_one = up_one.shape[1] - k_zero
    width = up_two.shape[0]
    quad = k_one // width
    family = (up_two.shape[1] - k_one) // up_root.shape[0]
    near = quad // 2
    pair = family // 2
    root_points = up_root.shape[1]

    far = pair // 2

    flux = jnp.einsum(
        "rlq,leq->rle",
        source,
        leaf_flux.reshape(leaves, edge_count, points),
        preferred_element_type=jnp.float32,
    )
    flux = rounded(flux).reshape(rhs_count, leaves * edge_count)
    box_state = rounded(contract(flux, box_up))
    first_sum = product(box_state[:, inner_dev:], up_one)

    roots = jnp.concatenate([up_root, down_root], axis=1)
    roots_far = swap(roots, far)
    first_sum = partner_sum(first_sum, 1)

    roots = joined_pair(roots, roots_far, place & far != 0, 0)
    roots_one = swap(roots, 1)
    first_sum = partner_sum(first_sum, near)
    first_state = rounded(first_sum)

    piece = lax.dynamic_slice_in_dim(first_state, k_zero + place % quad * width, width, 1)
    second_sum = product(piece, up_two)
    second_sum = partner_sum(second_sum, far | pair)
    second_sum, roots_one = lax.optimization_barrier((second_sum, roots_one))
    roots = joined_pair(roots, roots_one, place & 1 != 0, 1)
    up_part, down_part = roots[..., :root_points], roots[..., root_points:]
    up_near, up_pair = swap(up_part, near), swap(up_part, pair)
    second_sum = partner_sum(second_sum, near | pair)
    second_sum, up_near = lax.optimization_barrier((second_sum, up_near))
    down_near, down_pair = swap(down_part, near), swap(down_part, pair)
    up_high = swap(up_near, pair)
    down_high = swap(down_near, pair)
    second_sum = partner_sum(second_sum, 1 | pair)
    second_sum, up_high = lax.optimization_barrier((second_sum, up_high))
    second_sum = partner_sum(second_sum, pair)
    second_state = rounded(second_sum)
    up_rows = family_rows(up_part, up_near, up_pair, up_high, near, pair, place)
    down_rows = family_rows(down_part, down_near, down_pair, down_high, near, pair, place)

    root_sum = product(second_state[:, k_one:], up_rows)
    for bit in bits_of(family, count):
        root_sum = partner_sum(root_sum, bit | pair)
    root_state = rounded(root_sum)

    top_bound = rounded(contract(root_state, down_rows))
    second_input = jnp.concatenate([second_state[:, :k_one], top_bound], axis=1)
    mid_bound = rounded(contract(second_input, down_two))
    mid_bound = placed([mid_bound, swap(mid_bound, 1)], place, 1)
    mid_bound = placed([mid_bound, swap(mid_bound, near)], place // near, 1)
    first_input = jnp.concatenate([first_state[:, :k_zero], mid_bound], axis=1)

    box_bound = rounded(contract(first_input, down_one))
    box_input = jnp.concatenate([box_state[:, :inner_dev], box_bound], axis=1)
    leaf_bound = rounded(contract(box_input, box_down))
    edges = diagonal(leaf_bound[:, None, :], leaves)
    lifted = product(edges, leaf_lift)
    particular = jnp.einsum(
        "rlq,lqp->rlp",
        source,
        leaf_particular.reshape(leaves, points, points),
        preferred_element_type=jnp.float32,
    )
    return lifted.reshape(particular.shape) + particular


def solution(mesh):
    return jax.shard_map(
        per_device,
        mesh=mesh,
        in_specs=(P(None, AXES, None),) + (P(AXES, None),) * 11,
        out_specs=P(None, AXES, None),
        check_vma=False,
    )
```

```python
import jax
import jax.numpy as jnp
from jax import lax
from jax.sharding import PartitionSpec as P

AXES = ("gx", "gy")


def contract(left, right):
    return lax.dot_general(
        left, right, (((1,), (1,)), ((), ())), preferred_element_type=jnp.float32
    )


def product(left, right):
    return jnp.dot(left, right, preferred_element_type=jnp.float32)


def rounded(value):
    return value.astype(jnp.bfloat16)


def swap(value, mask):
    count = lax.axis_size(AXES)
    return lax.ppermute(value, AXES, [(i, i ^ mask) for i in range(count)])


def partner_sum(total, mask):
    return total + swap(rounded(total), mask).astype(jnp.float32)


def bits_of(first, last):
    bits = []
    while first < last:
        bits.append(first)
        first *= 2
    return bits


def placed(pieces, place, axis):
    bit = len(pieces) // 2
    if bit == 0:
        return pieces[0]
    low, high = placed(pieces[:bit], place, axis), placed(pieces[bit:], place, axis)
    upper = place & bit != 0
    return jnp.concatenate(
        [jnp.where(upper, high, low), jnp.where(upper, low, high)], axis=axis
    )


def joined_pair(joined, other, upper, axis):
    return jnp.stack(
        [jnp.where(upper, other, joined), jnp.where(upper, joined, other)], axis=axis
    )


def diagonal(rows, leaves):
    columns = rows.shape[2]
    leaf = jnp.arange(columns) // (columns // leaves)
    kept = jnp.where(leaf == jnp.arange(leaves)[:, None], rows, jnp.zeros((), rows.dtype))
    return kept.reshape(-1, columns)


def per_device(
    source,
    leaf_flux,
    leaf_particular,
    leaf_lift,
    box_up,
    box_down,
    up_one,
    down_one,
    up_two,
    down_two,
    up_root,
    down_root,
):
    rhs_count, leaves, points = source.shape
    edge_count = leaf_flux.shape[0] // leaves
    count = lax.axis_size(AXES)
    place = lax.axis_index(AXES)
    k_zero = up_one.shape[0]
    inner_dev = box_up.shape[0] - k_zero
    k_one = up_one.shape[1] - k_zero
    width = up_two.shape[0]
    quad = k_one // width
    family = (up_two.shape[1] - k_one) // up_root.shape[0]
    near = quad // 2
    pair = family // 2
    root_points = up_root.shape[1]

    far = pair // 2

    flux = jnp.einsum(
        "rlq,leq->rle",
        source,
        leaf_flux.reshape(leaves, edge_count, points),
        preferred_element_type=jnp.float32,
    )
    flux = rounded(flux).reshape(rhs_count, leaves * edge_count)
    box_state = rounded(contract(flux, box_up))
    first_sum = product(box_state[:, inner_dev:], up_one)

    roots = jnp.concatenate([up_root, down_root], axis=1)
    roots_far = swap(roots, far)
    first_sum = partner_sum(first_sum, 1)

    roots = joined_pair(roots, roots_far, place & far != 0, 0)
    roots_one = swap(roots, 1)
    first_sum = partner_sum(first_sum, near)
    first_state = rounded(first_sum)

    piece = lax.dynamic_slice_in_dim(first_state, k_zero + place % quad * width, width, 1)
    second_sum = product(piece, up_two)
    roots = joined_pair(roots, roots_one, place & 1 != 0, 1)
    roots_near, roots_pair = swap(roots, near), swap(roots, pair)
    second_sum = partner_sum(second_sum, far | pair)

    second_sum = partner_sum(second_sum, 1 | pair)
    low = joined_pair(roots, roots_near, place & near != 0, 1)
    high = swap(roots_near, pair)
    second_sum = partner_sum(second_sum, near | pair)
    kept = jnp.where(place < 0, -down_one, down_one)
    second_sum, high, kept = lax.optimization_barrier((second_sum, high, kept))
    high = joined_pair(roots_pair, high, place & near != 0, 1)
    second_sum = partner_sum(second_sum, pair)
    second_state = rounded(second_sum)
    roots = joined_pair(low, high, place & pair != 0, 0)
    roots = roots.reshape(-1, roots.shape[-1])

    root_sum = product(second_state[:, k_one:], roots[:, :root_points])
    for bit in bits_of(family, count):
        root_sum = partner_sum(root_sum, bit | pair)
    root_state = rounded(root_sum)

    top_bound = rounded(contract(root_state, roots[:, root_points:]))
    second_input = jnp.concatenate([second_state[:, :k_one], top_bound], axis=1)
    mid_bound = rounded(contract(second_input, down_two))
    mid_bound = placed([mid_bound, swap(mid_bound, 1)], place, 1)
    mid_bound = placed([mid_bound, swap(mid_bound, near)], place // near, 1)
    first_input = jnp.concatenate([first_state[:, :k_zero], mid_bound], axis=1)

    box_bound = rounded(contract(first_input, kept))
    box_input = jnp.concatenate([box_state[:, :inner_dev], box_bound], axis=1)
    leaf_bound = rounded(contract(box_input, box_down))
    edges = diagonal(leaf_bound[:, None, :], leaves)
    lifted = product(edges, leaf_lift)
    particular = jnp.einsum(
        "rlq,lqp->rlp",
        source,
        leaf_particular.reshape(leaves, points, points),
        preferred_element_type=jnp.float32,
    )
    return lifted.reshape(particular.shape) + particular


def solution(mesh):
    return jax.shard_map(
        per_device,
        mesh=mesh,
        in_specs=(P(None, AXES, None),) + (P(AXES, None),) * 11,
        out_specs=P(None, AXES, None),
        check_vma=False,
    )
```

```python
import jax
import jax.numpy as jnp
from jax import lax
from jax.sharding import PartitionSpec as P

AXES = ("gx", "gy")


def contract(left, right):
    return lax.dot_general(
        left, right, (((1,), (1,)), ((), ())), preferred_element_type=jnp.float32
    )


def product(left, right):
    return jnp.dot(left, right, preferred_element_type=jnp.float32)


def rounded(value):
    return value.astype(jnp.bfloat16)


def swap(value, mask):
    count = lax.axis_size(AXES)
    return lax.ppermute(value, AXES, [(i, i ^ mask) for i in range(count)])


def partner_sum(total, mask):
    return total + swap(rounded(total), mask).astype(jnp.float32)


def bits_of(first, last):
    bits = []
    while first < last:
        bits.append(first)
        first *= 2
    return bits


def placed(pieces, place, axis):
    bit = len(pieces) // 2
    if bit == 0:
        return pieces[0]
    low, high = placed(pieces[:bit], place, axis), placed(pieces[bit:], place, axis)
    upper = place & bit != 0
    return jnp.concatenate(
        [jnp.where(upper, high, low), jnp.where(upper, low, high)], axis=axis
    )


def joined_pair(joined, other, upper, axis):
    return jnp.stack(
        [jnp.where(upper, other, joined), jnp.where(upper, joined, other)], axis=axis
    )


def diagonal(rows, leaves):
    columns = rows.shape[2]
    leaf = jnp.arange(columns) // (columns // leaves)
    kept = jnp.where(leaf == jnp.arange(leaves)[:, None], rows, jnp.zeros((), rows.dtype))
    return kept.reshape(-1, columns)


def per_device(
    source,
    leaf_flux,
    leaf_particular,
    leaf_lift,
    box_up,
    box_down,
    up_one,
    down_one,
    up_two,
    down_two,
    up_root,
    down_root,
):
    rhs_count, leaves, points = source.shape
    edge_count = leaf_flux.shape[0] // leaves
    count = lax.axis_size(AXES)
    place = lax.axis_index(AXES)
    k_zero = up_one.shape[0]
    inner_dev = box_up.shape[0] - k_zero
    k_one = up_one.shape[1] - k_zero
    width = up_two.shape[0]
    quad = k_one // width
    family = (up_two.shape[1] - k_one) // up_root.shape[0]
    near = quad // 2
    pair = family // 2
    root_points = up_root.shape[1]

    far = pair // 2

    flux = jnp.einsum(
        "rlq,leq->rle",
        source,
        leaf_flux.reshape(leaves, edge_count, points),
        preferred_element_type=jnp.float32,
    )
    flux = rounded(flux).reshape(rhs_count, leaves * edge_count)
    box_state = rounded(contract(flux, box_up))
    first_sum = product(box_state[:, inner_dev:], up_one)

    roots = jnp.concatenate([up_root, down_root], axis=1)
    roots_far = swap(roots, far)
    first_sum = partner_sum(first_sum, 1)

    roots = joined_pair(roots, roots_far, place & far != 0, 0)
    roots_one = swap(roots, 1)
    first_sum = partner_sum(first_sum, near)
    first_state = rounded(first_sum)

    piece = lax.dynamic_slice_in_dim(first_state, k_zero + place % quad * width, width, 1)
    second_sum = product(piece, up_two)
    roots = joined_pair(roots, roots_one, place & 1 != 0, 1)
    roots_near, roots_pair = swap(roots, near), swap(roots, pair)
    second_sum = partner_sum(second_sum, far | pair)

    second_sum = partner_sum(second_sum, 1 | pair)
    low = joined_pair(roots, roots_near, place & near != 0, 1)
    high = swap(roots_near, pair)
    second_sum = partner_sum(second_sum, near | pair)
    kept = jnp.where(place < 0, -down_one, down_one)
    kept_down = jnp.where(place < 0, -box_down, box_down)
    second_sum, high, kept, kept_down = lax.optimization_barrier(
        (second_sum, high, kept, kept_down)
    )
    high = joined_pair(roots_pair, high, place & near != 0, 1)
    second_sum = partner_sum(second_sum, pair)
    second_state = rounded(second_sum)
    roots = joined_pair(low, high, place & pair != 0, 0)
    roots = roots.reshape(-1, roots.shape[-1])

    root_sum = product(second_state[:, k_one:], roots[:, :root_points])
    for bit in bits_of(family, count):
        root_sum = partner_sum(root_sum, bit | pair)
    root_state = rounded(root_sum)

    top_bound = rounded(contract(root_state, roots[:, root_points:]))
    second_input = jnp.concatenate([second_state[:, :k_one], top_bound], axis=1)
    mid_bound = rounded(contract(second_input, down_two))
    mid_bound = placed([mid_bound, swap(mid_bound, 1)], place, 1)
    mid_bound = placed([mid_bound, swap(mid_bound, near)], place // near, 1)
    first_input = jnp.concatenate([first_state[:, :k_zero], mid_bound], axis=1)

    box_bound = rounded(contract(first_input, kept))
    box_input = jnp.concatenate([box_state[:, :inner_dev], box_bound], axis=1)
    leaf_bound = rounded(contract(box_input, kept_down))
    edges = diagonal(leaf_bound[:, None, :], leaves)
    lifted = product(edges, leaf_lift)
    particular = jnp.einsum(
        "rlq,lqp->rlp",
        source,
        leaf_particular.reshape(leaves, points, points),
        preferred_element_type=jnp.float32,
    )
    return lifted.reshape(particular.shape) + particular


def solution(mesh):
    return jax.shard_map(
        per_device,
        mesh=mesh,
        in_specs=(P(None, AXES, None),) + (P(AXES, None),) * 11,
        out_specs=P(None, AXES, None),
        check_vma=False,
    )
```

```python
import jax
import jax.numpy as jnp
from jax import lax
from jax.sharding import PartitionSpec as P

AXES = ("gx", "gy")


def contract(left, right):
    return lax.dot_general(
        left, right, (((1,), (1,)), ((), ())), preferred_element_type=jnp.float32
    )


def product(left, right):
    return jnp.dot(left, right, preferred_element_type=jnp.float32)


def rounded(value):
    return value.astype(jnp.bfloat16)


def swap(value, mask):
    count = lax.axis_size(AXES)
    return lax.ppermute(value, AXES, [(i, i ^ mask) for i in range(count)])


def partner_sum(total, mask):
    return total + swap(rounded(total), mask).astype(jnp.float32)


def bits_of(first, last):
    bits = []
    while first < last:
        bits.append(first)
        first *= 2
    return bits


def placed(pieces, place, axis):
    bit = len(pieces) // 2
    if bit == 0:
        return pieces[0]
    low, high = placed(pieces[:bit], place, axis), placed(pieces[bit:], place, axis)
    upper = place & bit != 0
    return jnp.concatenate(
        [jnp.where(upper, high, low), jnp.where(upper, low, high)], axis=axis
    )


def joined_pair(joined, other, upper, axis):
    return jnp.stack(
        [jnp.where(upper, other, joined), jnp.where(upper, joined, other)], axis=axis
    )


def diagonal(rows, leaves):
    columns = rows.shape[2]
    leaf = jnp.arange(columns) // (columns // leaves)
    kept = jnp.where(leaf == jnp.arange(leaves)[:, None], rows, jnp.zeros((), rows.dtype))
    return kept.reshape(-1, columns)


def per_device(
    source,
    leaf_flux,
    leaf_particular,
    leaf_lift,
    box_up,
    box_down,
    up_one,
    down_one,
    up_two,
    down_two,
    up_root,
    down_root,
):
    rhs_count, leaves, points = source.shape
    edge_count = leaf_flux.shape[0] // leaves
    count = lax.axis_size(AXES)
    place = lax.axis_index(AXES)
    k_zero = up_one.shape[0]
    inner_dev = box_up.shape[0] - k_zero
    k_one = up_one.shape[1] - k_zero
    width = up_two.shape[0]
    quad = k_one // width
    family = (up_two.shape[1] - k_one) // up_root.shape[0]
    near = quad // 2
    pair = family // 2
    root_points = up_root.shape[1]

    far = pair // 2

    flux = jnp.einsum(
        "rlq,leq->rle",
        source,
        leaf_flux.reshape(leaves, edge_count, points),
        preferred_element_type=jnp.float32,
    )
    flux = rounded(flux).reshape(rhs_count, leaves * edge_count)
    box_state = rounded(contract(flux, box_up))
    first_sum = product(box_state[:, inner_dev:], up_one)

    roots = jnp.concatenate([up_root, down_root], axis=1)
    roots_far = swap(roots, far)
    first_sum = partner_sum(first_sum, 1)

    roots = joined_pair(roots, roots_far, place & far != 0, 0)
    roots_one = swap(roots, 1)
    first_sum = partner_sum(first_sum, near)
    first_state = rounded(first_sum)

    piece = lax.dynamic_slice_in_dim(first_state, k_zero + place % quad * width, width, 1)
    second_sum = product(piece, up_two)
    roots = joined_pair(roots, roots_one, place & 1 != 0, 1)
    roots_near, roots_pair = swap(roots, near), swap(roots, pair)
    second_sum = partner_sum(second_sum, far | pair)

    second_sum = partner_sum(second_sum, near | pair)
    low = joined_pair(roots, roots_near, place & near != 0, 1)
    high = swap(roots_near, pair)
    second_sum = partner_sum(second_sum, 1 | pair)
    second_sum, high = lax.optimization_barrier((second_sum, high))
    high = joined_pair(roots_pair, high, place & near != 0, 1)
    second_sum = partner_sum(second_sum, pair)
    second_state = rounded(second_sum)
    roots = joined_pair(low, high, place & pair != 0, 0)
    roots = roots.reshape(-1, roots.shape[-1])

    root_sum = product(second_state[:, k_one:], roots[:, :root_points])
    for bit in bits_of(family, count):
        root_sum = partner_sum(root_sum, bit | pair)
    root_state = rounded(root_sum)

    top_bound = rounded(contract(root_state, roots[:, root_points:]))
    second_input = jnp.concatenate([second_state[:, :k_one], top_bound], axis=1)
    mid_bound = rounded(contract(second_input, down_two))
    mid_bound = placed([mid_bound, swap(mid_bound, 1)], place, 1)
    mid_bound = placed([mid_bound, swap(mid_bound, near)], place // near, 1)
    first_input = jnp.concatenate([first_state[:, :k_zero], mid_bound], axis=1)

    box_bound = rounded(contract(first_input, down_one))
    box_input = jnp.concatenate([box_state[:, :inner_dev], box_bound], axis=1)
    leaf_bound = rounded(contract(box_input, box_down))
    edges = diagonal(leaf_bound[:, None, :], leaves)
    lifted = product(edges, leaf_lift)
    particular = jnp.einsum(
        "rlq,lqp->rlp",
        source,
        leaf_particular.reshape(leaves, points, points),
        preferred_element_type=jnp.float32,
    )
    return lifted.reshape(particular.shape) + particular


def solution(mesh):
    return jax.shard_map(
        per_device,
        mesh=mesh,
        in_specs=(P(None, AXES, None),) + (P(AXES, None),) * 11,
        out_specs=P(None, AXES, None),
        check_vma=False,
    )
```

```python
import jax
import jax.numpy as jnp
from jax import lax
from jax.sharding import PartitionSpec as P

AXES = ("gx", "gy")


def contract(left, right):
    return lax.dot_general(
        left, right, (((1,), (1,)), ((), ())), preferred_element_type=jnp.float32
    )


def product(left, right):
    return jnp.dot(left, right, preferred_element_type=jnp.float32)


def rounded(value):
    return value.astype(jnp.bfloat16)


def swap(value, mask):
    count = lax.axis_size(AXES)
    return lax.ppermute(value, AXES, [(i, i ^ mask) for i in range(count)])


def partner_sum(total, mask):
    return total + swap(rounded(total), mask).astype(jnp.float32)


def bits_of(first, last):
    bits = []
    while first < last:
        bits.append(first)
        first *= 2
    return bits


def placed(pieces, place, axis):
    bit = len(pieces) // 2
    if bit == 0:
        return pieces[0]
    low, high = placed(pieces[:bit], place, axis), placed(pieces[bit:], place, axis)
    upper = place & bit != 0
    return jnp.concatenate(
        [jnp.where(upper, high, low), jnp.where(upper, low, high)], axis=axis
    )


def joined_pair(joined, other, upper, axis):
    return jnp.stack(
        [jnp.where(upper, other, joined), jnp.where(upper, joined, other)], axis=axis
    )


def diagonal(rows, leaves):
    columns = rows.shape[2]
    leaf = jnp.arange(columns) // (columns // leaves)
    kept = jnp.where(leaf == jnp.arange(leaves)[:, None], rows, jnp.zeros((), rows.dtype))
    return kept.reshape(-1, columns)


def per_device(
    source,
    leaf_flux,
    leaf_particular,
    leaf_lift,
    box_up,
    box_down,
    up_one,
    down_one,
    up_two,
    down_two,
    up_root,
    down_root,
):
    rhs_count, leaves, points = source.shape
    edge_count = leaf_flux.shape[0] // leaves
    count = lax.axis_size(AXES)
    place = lax.axis_index(AXES)
    k_zero = up_one.shape[0]
    inner_dev = box_up.shape[0] - k_zero
    k_one = up_one.shape[1] - k_zero
    width = up_two.shape[0]
    quad = k_one // width
    family = (up_two.shape[1] - k_one) // up_root.shape[0]
    near = quad // 2
    pair = family // 2
    root_points = up_root.shape[1]

    far = pair // 2

    flux = jnp.einsum(
        "rlq,leq->rle",
        source,
        leaf_flux.reshape(leaves, edge_count, points),
        preferred_element_type=jnp.float32,
    )
    flux = rounded(flux).reshape(rhs_count, leaves * edge_count)
    box_state = rounded(contract(flux, box_up))
    first_sum = product(box_state[:, inner_dev:], up_one)

    roots = jnp.concatenate([up_root, down_root], axis=1)
    roots_far = swap(roots, far)
    first_sum = partner_sum(first_sum, 1)

    roots = joined_pair(roots, roots_far, place & far != 0, 0)
    roots_one = swap(roots, 1)
    first_sum = partner_sum(first_sum, near)
    first_state = rounded(first_sum)

    piece = lax.dynamic_slice_in_dim(first_state, k_zero + place % quad * width, width, 1)
    second_sum = product(piece, up_two)
    roots = joined_pair(roots, roots_one, place & 1 != 0, 1)
    roots_near, roots_pair = swap(roots, near), swap(roots, pair)
    second_sum = partner_sum(second_sum, near | pair)

    second_sum = partner_sum(second_sum, far | pair)
    low = joined_pair(roots, roots_near, place & near != 0, 1)
    high = swap(roots_near, pair)
    second_sum = partner_sum(second_sum, 1 | pair)
    second_sum, high = lax.optimization_barrier((second_sum, high))
    high = joined_pair(roots_pair, high, place & near != 0, 1)
    second_sum = partner_sum(second_sum, pair)
    second_state = rounded(second_sum)
    roots = joined_pair(low, high, place & pair != 0, 0)
    roots = roots.reshape(-1, roots.shape[-1])

    root_sum = product(second_state[:, k_one:], roots[:, :root_points])
    for bit in bits_of(family, count):
        root_sum = partner_sum(root_sum, bit | pair)
    root_state = rounded(root_sum)

    top_bound = rounded(contract(root_state, roots[:, root_points:]))
    second_input = jnp.concatenate([second_state[:, :k_one], top_bound], axis=1)
    mid_bound = rounded(contract(second_input, down_two))
    mid_bound = placed([mid_bound, swap(mid_bound, 1)], place, 1)
    mid_bound = placed([mid_bound, swap(mid_bound, near)], place // near, 1)
    first_input = jnp.concatenate([first_state[:, :k_zero], mid_bound], axis=1)

    box_bound = rounded(contract(first_input, down_one))
    box_input = jnp.concatenate([box_state[:, :inner_dev], box_bound], axis=1)
    leaf_bound = rounded(contract(box_input, box_down))
    edges = diagonal(leaf_bound[:, None, :], leaves)
    lifted = product(edges, leaf_lift)
    particular = jnp.einsum(
        "rlq,lqp->rlp",
        source,
        leaf_particular.reshape(leaves, points, points),
        preferred_element_type=jnp.float32,
    )
    return lifted.reshape(particular.shape) + particular


def solution(mesh):
    return jax.shard_map(
        per_device,
        mesh=mesh,
        in_specs=(P(None, AXES, None),) + (P(AXES, None),) * 11,
        out_specs=P(None, AXES, None),
        check_vma=False,
    )
```

```python
import jax
import jax.numpy as jnp
from jax import lax
from jax.sharding import PartitionSpec as P

AXES = ("gx", "gy")


def contract(left, right):
    return lax.dot_general(
        left, right, (((1,), (1,)), ((), ())), preferred_element_type=jnp.float32
    )


def product(left, right):
    return jnp.dot(left, right, preferred_element_type=jnp.float32)


def rounded(value):
    return value.astype(jnp.bfloat16)


def swap(value, mask):
    count = lax.axis_size(AXES)
    return lax.ppermute(value, AXES, [(i, i ^ mask) for i in range(count)])


def partner_sum(total, mask):
    return total + swap(rounded(total), mask).astype(jnp.float32)


def bits_of(first, last):
    bits = []
    while first < last:
        bits.append(first)
        first *= 2
    return bits


def placed(pieces, place, axis):
    bit = len(pieces) // 2
    if bit == 0:
        return pieces[0]
    low, high = placed(pieces[:bit], place, axis), placed(pieces[bit:], place, axis)
    upper = place & bit != 0
    return jnp.concatenate(
        [jnp.where(upper, high, low), jnp.where(upper, low, high)], axis=axis
    )


def joined_pair(joined, other, upper, axis):
    return jnp.stack(
        [jnp.where(upper, other, joined), jnp.where(upper, joined, other)], axis=axis
    )


def diagonal(rows, leaves):
    columns = rows.shape[2]
    leaf = jnp.arange(columns) // (columns // leaves)
    kept = jnp.where(leaf == jnp.arange(leaves)[:, None], rows, jnp.zeros((), rows.dtype))
    return kept.reshape(-1, columns)


def per_device(
    source,
    leaf_flux,
    leaf_particular,
    leaf_lift,
    box_up,
    box_down,
    up_one,
    down_one,
    up_two,
    down_two,
    up_root,
    down_root,
):
    rhs_count, leaves, points = source.shape
    edge_count = leaf_flux.shape[0] // leaves
    count = lax.axis_size(AXES)
    place = lax.axis_index(AXES)
    k_zero = up_one.shape[0]
    inner_dev = box_up.shape[0] - k_zero
    k_one = up_one.shape[1] - k_zero
    width = up_two.shape[0]
    quad = k_one // width
    family = (up_two.shape[1] - k_one) // up_root.shape[0]
    near = quad // 2
    pair = family // 2
    root_points = up_root.shape[1]

    far = pair // 2

    flux = jnp.einsum(
        "rlq,leq->rle",
        source,
        leaf_flux.reshape(leaves, edge_count, points),
        preferred_element_type=jnp.float32,
    )
    flux = rounded(flux).reshape(rhs_count, leaves * edge_count)
    box_state = rounded(contract(flux, box_up))
    first_sum = product(box_state[:, inner_dev:], up_one)

    roots = jnp.concatenate([up_root, down_root], axis=1)
    roots_far = swap(roots, far)
    first_sum = partner_sum(first_sum, 1)

    roots = joined_pair(roots, roots_far, place & far != 0, 0)
    roots_one = swap(roots, 1)
    first_sum = partner_sum(first_sum, near)
    first_state = rounded(first_sum)

    piece = lax.dynamic_slice_in_dim(first_state, k_zero + place % quad * width, width, 1)
    second_sum = product(piece, up_two)
    roots = joined_pair(roots, roots_one, place & 1 != 0, 1)
    roots_near, roots_pair = swap(roots, near), swap(roots, pair)
    second_sum = partner_sum(second_sum, far | pair)

    second_sum = partner_sum(second_sum, near | pair)
    low = joined_pair(roots, roots_near, place & near != 0, 1)
    high = swap(roots_near, pair)
    second_sum = partner_sum(second_sum, 1 | pair)
    second_sum, high = lax.optimization_barrier((second_sum, high))
    high = joined_pair(roots_pair, high, place & near != 0, 1)
    second_sum = partner_sum(second_sum, pair)
    second_state = rounded(second_sum)
    roots = joined_pair(low, high, place & pair != 0, 0)
    roots = roots.reshape(-1, roots.shape[-1])

    root_sum = product(second_state[:, k_one:], roots[:, :root_points])
    for bit in bits_of(family, count):
        root_sum = partner_sum(root_sum, bit | pair)
    root_state = rounded(root_sum)

    top_bound = rounded(contract(root_state, roots[:, root_points:]))
    second_input = jnp.concatenate([second_state[:, :k_one], top_bound], axis=1)
    mid_bound = rounded(contract(second_input, down_two))
    mid_bound = placed(
        [mid_bound] + [swap(mid_bound, mask) for mask in range(1, quad)], place, 1
    )
    first_input = jnp.concatenate([first_state[:, :k_zero], mid_bound], axis=1)

    box_bound = rounded(contract(first_input, down_one))
    box_input = jnp.concatenate([box_state[:, :inner_dev], box_bound], axis=1)
    leaf_bound = rounded(contract(box_input, box_down))
    edges = diagonal(leaf_bound[:, None, :], leaves)
    lifted = product(edges, leaf_lift)
    particular = jnp.einsum(
        "rlq,lqp->rlp",
        source,
        leaf_particular.reshape(leaves, points, points),
        preferred_element_type=jnp.float32,
    )
    return lifted.reshape(particular.shape) + particular


def solution(mesh):
    return jax.shard_map(
        per_device,
        mesh=mesh,
        in_specs=(P(None, AXES, None),) + (P(AXES, None),) * 11,
        out_specs=P(None, AXES, None),
        check_vma=False,
    )
```

```python
import jax
import jax.numpy as jnp
from jax import lax
from jax.sharding import PartitionSpec as P

AXES = ("gx", "gy")


def contract(left, right):
    return lax.dot_general(
        left, right, (((1,), (1,)), ((), ())), preferred_element_type=jnp.float32
    )


def product(left, right):
    return jnp.dot(left, right, preferred_element_type=jnp.float32)


def rounded(value):
    return value.astype(jnp.bfloat16)


def swap(value, mask):
    count = lax.axis_size(AXES)
    return lax.ppermute(value, AXES, [(i, i ^ mask) for i in range(count)])


def partner_sum(total, mask):
    return total + swap(rounded(total), mask).astype(jnp.float32)


def bits_of(first, last):
    bits = []
    while first < last:
        bits.append(first)
        first *= 2
    return bits


def placed(pieces, place, axis):
    bit = len(pieces) // 2
    if bit == 0:
        return pieces[0]
    low, high = placed(pieces[:bit], place, axis), placed(pieces[bit:], place, axis)
    upper = place & bit != 0
    return jnp.concatenate(
        [jnp.where(upper, high, low), jnp.where(upper, low, high)], axis=axis
    )


def joined_pair(joined, other, upper, axis):
    return jnp.stack(
        [jnp.where(upper, other, joined), jnp.where(upper, joined, other)], axis=axis
    )


def diagonal(rows, leaves):
    columns = rows.shape[2]
    leaf = jnp.arange(columns) // (columns // leaves)
    kept = jnp.where(leaf == jnp.arange(leaves)[:, None], rows, jnp.zeros((), rows.dtype))
    return kept.reshape(-1, columns)


def per_device(
    source,
    leaf_flux,
    leaf_particular,
    leaf_lift,
    box_up,
    box_down,
    up_one,
    down_one,
    up_two,
    down_two,
    up_root,
    down_root,
):
    rhs_count, leaves, points = source.shape
    edge_count = leaf_flux.shape[0] // leaves
    count = lax.axis_size(AXES)
    place = lax.axis_index(AXES)
    k_zero = up_one.shape[0]
    inner_dev = box_up.shape[0] - k_zero
    k_one = up_one.shape[1] - k_zero
    width = up_two.shape[0]
    quad = k_one // width
    family = (up_two.shape[1] - k_one) // up_root.shape[0]
    near = quad // 2
    pair = family // 2
    root_points = up_root.shape[1]

    far = pair // 2

    flux = jnp.einsum(
        "rlq,leq->rle",
        source,
        leaf_flux.reshape(leaves, edge_count, points),
        preferred_element_type=jnp.float32,
    )
    flux = rounded(flux).reshape(rhs_count, leaves * edge_count)
    box_state = rounded(contract(flux, box_up))
    first_sum = product(box_state[:, inner_dev:], up_one)

    roots = jnp.concatenate([up_root, down_root], axis=1)
    roots_far = swap(roots, far)
    first_sum = partner_sum(first_sum, 1)

    roots = joined_pair(roots, roots_far, place & far != 0, 0)
    roots = swap(swap(roots, pair), pair)
    roots_one = swap(roots, 1)
    first_sum = partner_sum(first_sum, near)
    first_state = rounded(first_sum)

    piece = lax.dynamic_slice_in_dim(first_state, k_zero + place % quad * width, width, 1)
    second_sum = product(piece, up_two)
    roots = joined_pair(roots, roots_one, place & 1 != 0, 1)
    roots_near, roots_pair = swap(roots, near), swap(roots, pair)
    second_sum = partner_sum(second_sum, far | pair)

    second_sum = partner_sum(second_sum, near | pair)
    low = joined_pair(roots, roots_near, place & near != 0, 1)
    high = swap(roots_near, pair)
    second_sum = partner_sum(second_sum, 1 | pair)
    second_sum, high = lax.optimization_barrier((second_sum, high))
    high = joined_pair(roots_pair, high, place & near != 0, 1)
    second_sum = partner_sum(second_sum, pair)
    second_state = rounded(second_sum)
    roots = joined_pair(low, high, place & pair != 0, 0)
    roots = roots.reshape(-1, roots.shape[-1])

    root_sum = product(second_state[:, k_one:], roots[:, :root_points])
    for bit in bits_of(family, count):
        root_sum = partner_sum(root_sum, bit | pair)
    root_state = rounded(root_sum)

    top_bound = rounded(contract(root_state, roots[:, root_points:]))
    second_input = jnp.concatenate([second_state[:, :k_one], top_bound], axis=1)
    mid_bound = rounded(contract(second_input, down_two))
    mid_bound = placed([mid_bound, swap(mid_bound, 1)], place, 1)
    mid_bound = placed([mid_bound, swap(mid_bound, near)], place // near, 1)
    first_input = jnp.concatenate([first_state[:, :k_zero], mid_bound], axis=1)

    box_bound = rounded(contract(first_input, down_one))
    box_input = jnp.concatenate([box_state[:, :inner_dev], box_bound], axis=1)
    leaf_bound = rounded(contract(box_input, box_down))
    edges = diagonal(leaf_bound[:, None, :], leaves)
    lifted = product(edges, leaf_lift)
    particular = jnp.einsum(
        "rlq,lqp->rlp",
        source,
        leaf_particular.reshape(leaves, points, points),
        preferred_element_type=jnp.float32,
    )
    return lifted.reshape(particular.shape) + particular


def solution(mesh):
    return jax.shard_map(
        per_device,
        mesh=mesh,
        in_specs=(P(None, AXES, None),) + (P(AXES, None),) * 11,
        out_specs=P(None, AXES, None),
        check_vma=False,
    )
```

```python
import jax
import jax.numpy as jnp
from jax import lax
from jax.sharding import PartitionSpec as P

AXES = ("gx", "gy")


def contract(left, right):
    return lax.dot_general(
        left, right, (((1,), (1,)), ((), ())), preferred_element_type=jnp.float32
    )


def product(left, right):
    return jnp.dot(left, right, preferred_element_type=jnp.float32)


def rounded(value):
    return value.astype(jnp.bfloat16)


def swap(value, mask):
    count = lax.axis_size(AXES)
    return lax.ppermute(value, AXES, [(i, i ^ mask) for i in range(count)])


def partner_sum(total, mask):
    return total + swap(rounded(total), mask).astype(jnp.float32)


def bits_of(first, last):
    bits = []
    while first < last:
        bits.append(first)
        first *= 2
    return bits


def placed(pieces, place, axis):
    bit = len(pieces) // 2
    if bit == 0:
        return pieces[0]
    low, high = placed(pieces[:bit], place, axis), placed(pieces[bit:], place, axis)
    upper = place & bit != 0
    return jnp.concatenate(
        [jnp.where(upper, high, low), jnp.where(upper, low, high)], axis=axis
    )


def joined_pair(joined, other, upper, axis):
    return jnp.stack(
        [jnp.where(upper, other, joined), jnp.where(upper, joined, other)], axis=axis
    )


def diagonal(rows, leaves):
    columns = rows.shape[2]
    leaf = jnp.arange(columns) // (columns // leaves)
    kept = jnp.where(leaf == jnp.arange(leaves)[:, None], rows, jnp.zeros((), rows.dtype))
    return kept.reshape(-1, columns)


def per_device(
    source,
    leaf_flux,
    leaf_particular,
    leaf_lift,
    box_up,
    box_down,
    up_one,
    down_one,
    up_two,
    down_two,
    up_root,
    down_root,
):
    rhs_count, leaves, points = source.shape
    edge_count = leaf_flux.shape[0] // leaves
    count = lax.axis_size(AXES)
    place = lax.axis_index(AXES)
    k_zero = up_one.shape[0]
    inner_dev = box_up.shape[0] - k_zero
    k_one = up_one.shape[1] - k_zero
    width = up_two.shape[0]
    quad = k_one // width
    family = (up_two.shape[1] - k_one) // up_root.shape[0]
    near = quad // 2
    pair = family // 2
    root_points = up_root.shape[1]

    far = pair // 2

    every = contract(source.reshape(-1, points), leaf_flux)
    every = every.reshape(rhs_count, leaves, leaves * edge_count)
    owner = jnp.arange(leaves * edge_count) // edge_count
    own = owner == jnp.arange(leaves)[:, None]
    flux = rounded(jnp.sum(jnp.where(own, every, 0.0), axis=1))
    box_state = rounded(contract(flux, box_up))
    first_sum = product(box_state[:, inner_dev:], up_one)

    roots = jnp.concatenate([up_root, down_root], axis=1)
    roots_far = swap(roots, far)
    first_sum = partner_sum(first_sum, 1)

    roots = joined_pair(roots, roots_far, place & far != 0, 0)
    roots_one = swap(roots, 1)
    first_sum = partner_sum(first_sum, near)
    first_state = rounded(first_sum)

    piece = lax.dynamic_slice_in_dim(first_state, k_zero + place % quad * width, width, 1)
    second_sum = product(piece, up_two)
    roots = joined_pair(roots, roots_one, place & 1 != 0, 1)
    roots_near, roots_pair = swap(roots, near), swap(roots, pair)
    second_sum = partner_sum(second_sum, far | pair)

    second_sum = partner_sum(second_sum, near | pair)
    low = joined_pair(roots, roots_near, place & near != 0, 1)
    high = swap(roots_near, pair)
    second_sum = partner_sum(second_sum, 1 | pair)
    second_sum, high = lax.optimization_barrier((second_sum, high))
    high = joined_pair(roots_pair, high, place & near != 0, 1)
    second_sum = partner_sum(second_sum, pair)
    second_state = rounded(second_sum)
    roots = joined_pair(low, high, place & pair != 0, 0)
    roots = roots.reshape(-1, roots.shape[-1])

    root_sum = product(second_state[:, k_one:], roots[:, :root_points])
    for bit in bits_of(family, count):
        root_sum = partner_sum(root_sum, bit | pair)
    root_state = rounded(root_sum)

    top_bound = rounded(contract(root_state, roots[:, root_points:]))
    second_input = jnp.concatenate([second_state[:, :k_one], top_bound], axis=1)
    mid_bound = rounded(contract(second_input, down_two))
    mid_bound = placed([mid_bound, swap(mid_bound, 1)], place, 1)
    mid_bound = placed([mid_bound, swap(mid_bound, near)], place // near, 1)
    first_input = jnp.concatenate([first_state[:, :k_zero], mid_bound], axis=1)

    box_bound = rounded(contract(first_input, down_one))
    box_input = jnp.concatenate([box_state[:, :inner_dev], box_bound], axis=1)
    leaf_bound = rounded(contract(box_input, box_down))
    edges = diagonal(leaf_bound[:, None, :], leaves)
    lifted = product(edges, leaf_lift)
    particular = jnp.einsum(
        "rlq,lqp->rlp",
        source,
        leaf_particular.reshape(leaves, points, points),
        preferred_element_type=jnp.float32,
    )
    return lifted.reshape(particular.shape) + particular


def solution(mesh):
    return jax.shard_map(
        per_device,
        mesh=mesh,
        in_specs=(P(None, AXES, None),) + (P(AXES, None),) * 11,
        out_specs=P(None, AXES, None),
        check_vma=False,
    )
```
